256 devices in a mesh: pix: 16 (over y, x), tm: 16 (over z, core).
Axes of the slice: x: 4, y: 4, z: 8, core: 2. Of those that a mesh axis runs over, the one named last changes fastest.
Arguments:
- movie: bfloat16 [320, 128, 2048], P('pix', None, 'tm'), may hold values from -6 to 6
- noise_weight: float32 [320, 128], P('pix'), may hold values from 0.25 to 4
- footprints: bfloat16 [320, 4, 128, 512], P('pix')
- block_ids: int32 [320, 4], P('pix'), may hold values from 0 to 31, as said below
- band_width: int32 [1024], replicated, may hold values from 0 to 5, as said below
- precision_blocks: bfloat16 [11, 128, 128], replicated
Outputs:
- traces: bfloat16 [16384, 2048], P('pix', 'tm')
- residual: bfloat16 [320, 128, 2048], P('pix', None, 'tm')
The draws below stay inside these ranges and needn't reach their ends.
Inputs may be any that keep to these rules, and one draw needn't show every extreme that they name: `block_ids`: each tile names 4 different component blocks. `band_width`: some group has the reach 5.
All inputs are finite; a program needn't handle non-finite values.
Results may differ from the reference program's by a relative error of at most 0.015.
Values may be sent and summed in bfloat16 or wider, within the bound.
No kernel may reach another device: no remote copies, remote signals or barrier semaphores. Data moves between devices by JAX's collectives and lax.ppermute only.
A program may use at most 128 MiB of HBM per device.

```python
import math
import jax
import jax.numpy as jnp
from jax import lax

K = 16384
CBLK = 512
TILE = 128
SLOTS = 4
GROUP = 16
BMAX = 5
FR = 128
TILES = 320
T_SIZE = 2048
KB = 32
NG = 1024
GROUPS_DEV = 4
N_PIX = 16


def draw_footprints(key, part):
    scale_top = (3.0 * KB / (TILE * TILES * SLOTS)) ** 0.5
    shape_all = (TILES, SLOTS, TILE, CBLK)
    key_value, key_keep = jax.random.split(jax.random.fold_in(key, 17))
    values = jax.random.uniform(key_value, shape_all, jnp.float32, 0.0, 1.0)
    kept = jax.random.bernoulli(key_keep, 0.1, shape_all).astype(jnp.float32)
    return (values * kept * 10.0 ** 0.5 * scale_top).astype(jnp.bfloat16)


def draw_block_ids(key, part):
    tile_keys = jax.random.split(key, TILES)

    def one_tile(tile_key):
        return jax.random.permutation(tile_key, KB)[:SLOTS]
    return jax.vmap(one_tile)(tile_keys).astype(jnp.int32)


def draw_band_width(key, part):
    key_base, key_hot, key_forced = jax.random.split(key, 3)
    base_reach = jax.random.randint(key_base, (NG,), 0, 3)
    hot_ranges = jax.random.randint(key_hot, (NG // GROUPS_DEV,), 0, 4) == 0
    hot_groups = jnp.repeat(hot_ranges, GROUPS_DEV)
    widths = jnp.where(hot_groups, BMAX, base_reach)
    forced = jax.random.randint(key_forced, (), 0, NG)
    return widths.at[forced].set(BMAX).astype(jnp.int32)


def draw_precision_blocks(key, part):
    offset_count = 2 * BMAX + 1
    offsets = jnp.abs(jnp.arange(offset_count) - BMAX).astype(jnp.float32)
    decay_scale = (0.7 ** offsets)[:, None, None]
    random_part = jax.random.normal(key, (offset_count, FR, FR), jnp.float32)
    blocks = decay_scale * random_part / FR ** 0.5
    identity = jnp.eye(FR, dtype=jnp.float32)
    center = (offsets == 0).astype(jnp.float32)[:, None, None]
    return (blocks + center * identity).astype(jnp.bfloat16)


def shard_levels(key, dims, cuts, smallest, largest):
    gain = 1.0
    for axis_at, blocks in cuts:
        steps = jax.random.uniform(jax.random.fold_in(jax.random.fold_in(key, 6), axis_at), (blocks,), jnp.float32, smallest / len(cuts), largest / len(cuts))
        gain = gain * jnp.repeat(jnp.exp(steps), dims[axis_at] // blocks).reshape((-1,) + (1,) * (len(dims) - 1 - axis_at))
    return gain


def gaussian(rng, dims, deviation, reach, cuts=(), held_as=jnp.bfloat16):
    level = shard_levels(rng, dims, cuts, -0.22, 0.18) if cuts else 1.0
    entries = jax.random.normal(rng, dims, jnp.float32) * deviation * level
    return jnp.minimum(jnp.maximum(entries, -reach), reach).astype(held_as)


def setup_inputs(seed: int = 0) -> dict:
    keys = jax.random.split(jax.random.key(seed), 7)
    return {
        "movie": gaussian(keys[0], (TILES, TILE, T_SIZE), 1.0, 6.0, ((0, 16), (2, 16))),
        "noise_weight": jnp.clip(jnp.exp(math.log(4.0) - 2.7725887 * jax.random.uniform(keys[1], (TILES, TILE), jnp.float32) ** shard_levels(keys[1], (TILES, TILE), ((0, 16),), -0.2, 0.2)), 0.25, 4.0),
        "footprints": draw_footprints(jax.random.fold_in(keys[6], 71), 0),
        "block_ids": draw_block_ids(jax.random.fold_in(keys[6], 71), 0),
        "band_width": draw_band_width(jax.random.fold_in(keys[6], 71), 0),
        "precision_blocks": draw_precision_blocks(jax.random.fold_in(keys[6], 71), 0),
    }


def reference(movie, noise_weight, footprints, block_ids, band_width, precision_blocks):
    frames = movie.shape[2]
    weighted = (noise_weight[:, :, None] * movie.astype(jnp.float32)).astype(jnp.bfloat16)

    def project(running, item):
        feet, idents, pixels = item
        contrib = jnp.einsum('spc,pf->scf', feet.astype(jnp.float32), pixels.astype(jnp.float32))
        return running.at[idents].add(contrib), None

    def one_index(total, item):
        feet, idents, pixels = item
        start = jnp.zeros((K // CBLK, CBLK, frames), jnp.float32)
        part_sum, _ = lax.scan(project, start, (feet, idents, pixels))
        rounded = lax.optimization_barrier(part_sum.astype(jnp.bfloat16)).astype(jnp.float32)
        return total + rounded, None

    tiles_all = movie.shape[0]
    per_index = tiles_all // N_PIX
    grouped = (footprints.reshape(N_PIX, per_index, SLOTS, TILE, CBLK),
               block_ids.reshape(N_PIX, per_index, SLOTS),
               weighted.reshape(N_PIX, per_index, TILE, frames))
    initial = jnp.zeros((K // CBLK, CBLK, frames), jnp.float32)
    summed, _ = lax.scan(one_index, initial, grouped)
    projected = summed.reshape(K, frames).astype(jnp.bfloat16)
    nblocks = frames // FR
    blocks = projected.astype(jnp.float32).reshape(K, nblocks, FR)
    padded = jnp.pad(blocks, ((0, 0), (BMAX, BMAX), (0, 0)))
    widths = jnp.repeat(band_width, GROUP)
    filtered = jnp.zeros((K, nblocks, FR), jnp.float32)
    for offset in range(-BMAX, BMAX + 1):
        shifted = padded[:, BMAX + offset:BMAX + offset + nblocks, :]
        term = jnp.einsum('kbf,fh->kbh', shifted, precision_blocks[offset + BMAX].astype(jnp.float32))
        inside = (abs(offset) <= widths).astype(jnp.float32)
        filtered = filtered + inside[:, None, None] * term
    traces = filtered.reshape(K, frames).astype(jnp.bfloat16)
    trace_blocks = traces.reshape(K // CBLK, CBLK, frames)

    def rebuild(item):
        feet, idents, pixels = item
        chosen = trace_blocks[idents].astype(jnp.float32)
        rebuilt = jnp.einsum('spc,scf->pf', feet.astype(jnp.float32), chosen)
        return (pixels.astype(jnp.float32) - rebuilt).astype(jnp.bfloat16)

    residual = lax.map(rebuild, (footprints, block_ids, movie))
    return traces, residual
```

```python
import functools

import jax
import jax.numpy as jnp
from jax import lax
from jax.experimental import pallas as pl
from jax.experimental.pallas import tpu as pltpu
from jax.sharding import Mesh
from jax.sharding import PartitionSpec as P

K = 16384
CBLK = 512
KB = 32
TILE = 128
SLOTS = 4
GROUP = 16
BMAX = 5
FR = 128
SIDE = 4
STEP = 4
f32 = jnp.float32
bf16 = jnp.bfloat16


def near(target, here):
    d = (target - here) & 3
    return d ^ (d >> 1)


def place(block, y, x):
    owner, half = block >> 1, block & 1
    ny, nx = near(owner >> 2, y), near(owner & 3, x)
    return jnp.where(half == 0, ny * 4 + nx, 16 + nx * 4 + ny)


def project_kernel(ids, movie, noise, feet, *rest):
    outs, acc = rest[:-1], rest[-1]
    n = pl.program_id(0)
    y, x = lax.axis_index("y"), lax.axis_index("x")

    @pl.when(n == 0)
    def _():
        acc[...] = jnp.zeros_like(acc)

    for i in range(STEP):
        w = (noise[i].reshape(TILE, 1) * movie[i].astype(f32)).astype(bf16)
        for s in range(SLOTS):
            b = place(ids[n * STEP + i, s], y, x)
            acc[b] += lax.dot_general(
                feet[i, s], w, (((0,), (0,)), ((), ())), preferred_element_type=f32
            )

    @pl.when(n == pl.num_programs(0) - 1)
    def _():
        at = 0
        for out in outs:
            k = out.shape[0] // CBLK
            out[...] = acc[at : at + k].reshape(out.shape).astype(bf16)
            at += k


def project(movie, noise, feet, ids):
    tiles = movie.shape[0]
    sizes = (4, 2, 2, 2, 2, 2, 2) * 2
    return pl.pallas_call(
        project_kernel,
        grid_spec=pltpu.PrefetchScalarGridSpec(
            num_scalar_prefetch=1,
            grid=(tiles // STEP,),
            in_specs=[
                pl.BlockSpec((STEP, TILE, FR), lambda n, i: (n, 0, 0)),
                pl.BlockSpec((STEP, 1, TILE), lambda n, i: (n, 0, 0)),
                pl.BlockSpec((STEP, SLOTS, TILE, CBLK), lambda n, i: (n, 0, 0, 0)),
            ],
            out_specs=[pl.BlockSpec((k * CBLK, FR), lambda n, i: (0, 0)) for k in sizes],
            scratch_shapes=[pltpu.VMEM((KB, CBLK, FR), f32)],
        ),
        out_shape=[jax.ShapeDtypeStruct((k * CBLK, FR), bf16) for k in sizes],
        compiler_params=pltpu.CompilerParams(vmem_limit_bytes=40 * 2**20),
        cost_estimate=pl.CostEstimate(flops=1342177280, bytes_accessed=15000000, transcendentals=0),
    )(ids, movie, noise[:, None, :], feet)


def filter_kernel(bw, x, prec, out, pad, acc):
    nb, rows, _ = x.shape
    per = rows // GROUP
    base = lax.axis_index("y")
    for name in ("x", "z", "c"):
        base = base * lax.axis_size(name) + lax.axis_index(name)
    base = base * per
    pad[:BMAX] = jnp.zeros((BMAX, rows, FR), bf16)
    pad[BMAX + nb :] = jnp.zeros((BMAX, rows, FR), bf16)
    pad[BMAX : BMAX + nb] = x[...]
    reach = jnp.concatenate(
        [jnp.full((1, GROUP, FR), bw[base + g], jnp.int32) for g in range(per)], axis=1
    )
    for d in range(-BMAX, BMAX + 1):
        src = pad[BMAX + d : BMAX + d + nb].reshape(nb * rows, FR)
        term = jnp.dot(src, prec[d + BMAX], preferred_element_type=f32).reshape(nb, rows, FR)
        term = jnp.where(reach >= abs(d), term, 0.0)
        if d == -BMAX:
            acc[...] = term
        else:
            acc[...] += term
    out[...] = acc[...].astype(bf16)


def band_filter(x, bw, prec):
    nb, rows, _ = x.shape
    return pl.pallas_call(
        filter_kernel,
        in_specs=[
            pl.BlockSpec(memory_space=pltpu.SMEM),
            pl.BlockSpec(memory_space=pltpu.VMEM),
            pl.BlockSpec(memory_space=pltpu.VMEM),
        ],
        out_specs=pl.BlockSpec(memory_space=pltpu.VMEM),
        out_shape=jax.ShapeDtypeStruct(x.shape, bf16),
        scratch_shapes=[
            pltpu.VMEM((nb + 2 * BMAX, rows, FR), bf16),
            pltpu.VMEM((nb, rows, FR), f32),
        ],
        cost_estimate=pl.CostEstimate(flops=369000000, bytes_accessed=800000, transcendentals=0),
    )(bw, x, prec)


def rebuild_kernel(ids, movie, feet, *rest):
    parts, out, held, sems = rest[:-3], rest[-3], rest[-2], rest[-1]
    n = pl.program_id(0)
    y, x = lax.axis_index("y"), lax.axis_index("x")

    @pl.when(n == 0)
    def _():
        copies, at = [], 0
        for k, part in enumerate(parts):
            rows = part.shape[0]
            copies.append(
                pltpu.make_async_copy(part, held.at[pl.ds(at, rows)], sems.at[k])
            )
            at += rows
        for copy in copies:
            copy.start()
        for copy in copies:
            copy.wait()

    for i in range(STEP):
        total = movie[i].astype(f32)
        for s in range(SLOTS):
            b = place(ids[n * STEP + i, s], y, x)
            rows = pl.ds(pl.multiple_of(b * CBLK, CBLK), CBLK)
            total -= jnp.dot(feet[i, s], held[rows, :], preferred_element_type=f32)
        out[i] = total.astype(bf16)


def rebuild(movie, feet, ids, parts):
    tiles = movie.shape[0]
    return pl.pallas_call(
        rebuild_kernel,
        grid_spec=pltpu.PrefetchScalarGridSpec(
            num_scalar_prefetch=1,
            grid=(tiles // STEP,),
            in_specs=[
                pl.BlockSpec((STEP, TILE, FR), lambda n, i: (n, 0, 0)),
                pl.BlockSpec((STEP, SLOTS, TILE, CBLK), lambda n, i: (n, 0, 0, 0)),
            ]
            + [pl.BlockSpec(memory_space=pl.ANY)] * len(parts),
            out_specs=pl.BlockSpec((STEP, TILE, FR), lambda n, i: (n, 0, 0)),
            scratch_shapes=[
                pltpu.VMEM((K, FR), bf16),
                pltpu.SemaphoreType.DMA((len(parts),)),
            ],
        ),
        out_shape=jax.ShapeDtypeStruct(movie.shape, bf16),
        compiler_params=pltpu.CompilerParams(vmem_limit_bytes=40 * 2**20),
        cost_estimate=pl.CostEstimate(flops=1342177280, bytes_accessed=16000000, transcendentals=0),
    )(ids, movie, feet, *parts)


def shift(v, axis, k):
    n = lax.axis_size(axis)
    return lax.ppermute(v, axis, [(i, (i + k) % n) for i in range(n)])


def add(*terms):
    total = terms[0].astype(f32)
    for term in terms[1:]:
        total = total + term.astype(f32)
    return total.astype(bf16)


def reduce_ring(own, up_lo, up_hi, down_lo, down_hi, far_lo, far_hi, axis):
    far_up = shift(far_lo, axis, 1)
    far_down = shift(far_hi, axis, -1)
    got_hi = shift(up_hi, axis, 1)
    got_lo = shift(down_lo, axis, -1)
    late_lo = shift(add(up_lo, far_up), axis, 1)
    late_hi = shift(add(down_hi, far_down), axis, -1)
    h = own.shape[0] // 2
    return add(own[:h], got_lo, late_lo), add(own[h:], got_hi, late_hi)


def reduce_plane(pieces, first, second):
    lo, hi = reduce_ring(*pieces, first)
    n = lo.shape[0] // 2
    h = n // 2
    own, up, down, far = lo[:n], lo[n:], hi[:n], hi[n:]
    return reduce_ring(own, up[:h], up[h:], down[:h], down[h:], far[:h], far[h:], second)


def gather_ring(v, axis):
    h = v.shape[0] // 2
    up, down = shift(v, axis, -1), shift(v, axis, 1)
    far_lo, far_hi = shift(down[:h], axis, 1), shift(up[h:], axis, -1)
    return v, up, down, far_lo, far_hi


def gather_plane(v, first, second):
    row = jnp.concatenate(gather_ring(v, first), axis=0)
    return gather_ring(row, second)


def shards(movie, noise_weight, footprints, block_ids, band_width, precision_blocks):
    tm = ("z", "c")
    nb = lax.axis_size("z") * lax.axis_size("c")
    pieces = project(movie, noise_weight, footprints, block_ids)
    even = reduce_plane(pieces[:7], "y", "x")
    odd = reduce_plane(pieces[7:], "x", "y")
    projected = jnp.concatenate(even + odd, axis=0)
    rows = projected.shape[0]
    regrouped = lax.all_to_all(projected.reshape(nb, rows // nb, FR), tm, 0, 0, tiled=True)
    filtered = band_filter(regrouped, band_width, precision_blocks)
    traces = lax.all_to_all(filtered, tm, 0, 0, tiled=True).reshape(rows, FR)
    parts = gather_plane(traces[:CBLK], "x", "y")
    parts_odd = gather_plane(traces[CBLK:], "y", "x")
    residual = rebuild(movie, footprints, block_ids, parts + parts_odd)
    return traces, residual


def solution(mesh):
    devices = mesh.devices.reshape(SIDE, SIDE, mesh.devices.shape[1] // 2, 2)
    grid = Mesh(devices, ("y", "x", "z", "c"))
    pix, tm = ("y", "x"), ("z", "c")
    return jax.shard_map(
        shards,
        mesh=grid,
        in_specs=(
            P(pix, None, tm),
            P(pix, None),
            P(pix, None, None, None),
            P(pix, None),
            P(),
            P(),
        ),
        out_specs=(P(pix, tm), P(pix, None, tm)),
        check_vma=False,
    )
```

```python
import functools

import jax
import jax.numpy as jnp
from jax import lax
from jax.experimental import pallas as pl
from jax.experimental.pallas import tpu as pltpu
from jax.sharding import Mesh
from jax.sharding import PartitionSpec as P

CBLK = 512
TILE = 128
SLOTS = 4
GROUP = 16
BMAX = 5
FR = 128
WIDE = 2 * FR
SIDE = 4
OWNED = SIDE * SIDE
f32 = jnp.float32
bf16 = jnp.bfloat16
UNROLL = 4
AXES = ("y", "x", "z", "c")


def near(target, here):
    d = (target - here) & 3
    return d ^ (d >> 1)


def places_of(block_ids):
    y, x, c = lax.axis_index("y"), lax.axis_index("x"), lax.axis_index("c")
    owner = block_ids >> 1
    ny, nx = near(owner >> 2, y), near(owner & 3, x)
    at = jnp.where(c == 0, ny * 4 + nx, nx * 4 + ny)
    return jnp.where((block_ids & 1) == c, at, -1).reshape(-1)


def start_slots(places, feet, buf, sems, slot_of, place_of, low, high):
    def scan(i, count):
        at = places[i]
        wanted = (at >= low) & (at < high)

        @pl.when(wanted)
        def _():
            slot_of[count] = i
            place_of[count] = at - low
            pltpu.make_async_copy(feet.at[i], buf.at[count], sems.at[count]).start()

        return count + wanted.astype(jnp.int32)

    count = lax.fori_loop(0, places.shape[0], scan, 0)
    for k in range(UNROLL - 1):
        slot_of[count + k] = 0
        place_of[count + k] = high - low
    return count


def wait_slots(j, count, feet, buf, sems, slot_of):
    for k in range(UNROLL):

        @pl.when(j + k < count)
        def _():
            pltpu.make_async_copy(feet.at[slot_of[j + k]], buf.at[j + k], sems.at[j + k]).wait()


def project_kernel(places, own, other, feet, *rest, low, high):
    outs = rest[:-5]
    buf, sems, slot_of, place_of, acc = rest[-5:]
    count = start_slots(places, feet, buf, sems, slot_of, place_of, low, high)
    acc[...] = jnp.zeros_like(acc)

    def some(g, carry):
        j = g * UNROLL
        wait_slots(j, count, feet, buf, sems, slot_of)
        for k in range(UNROLL):
            n = slot_of[j + k] // SLOTS
            w = jnp.concatenate([own[n], other[n]], axis=1)
            acc[place_of[j + k]] += lax.dot_general(
                buf[j + k], w, (((0,), (0,)), ((), ())), preferred_element_type=f32
            )
        return carry

    lax.fori_loop(0, (count + UNROLL - 1) // UNROLL, some, 0)
    at = 0
    for out in outs:
        k = out.shape[0] // CBLK
        out[...] = acc[at : at + k].reshape(out.shape).astype(bf16)
        at += k


def project(own, other, feet, places, low, sizes):
    slots = places.shape[0]
    room = slots + UNROLL - 1
    total = sum(sizes)
    vmem = pl.BlockSpec(memory_space=pltpu.VMEM)
    return pl.pallas_call(
        functools.partial(project_kernel, low=low, high=low + total),
        in_specs=[
            pl.BlockSpec(memory_space=pltpu.SMEM), vmem, vmem,
            pl.BlockSpec(memory_space=pl.ANY),
        ],
        out_specs=[vmem] * len(sizes),
        scratch_shapes=[
            pltpu.VMEM((room, TILE, CBLK), bf16),
            pltpu.SemaphoreType.DMA((slots,)),
            pltpu.SMEM((room,), jnp.int32),
            pltpu.SMEM((room,), jnp.int32),
            pltpu.VMEM((total + 1, CBLK, WIDE), f32),
        ],
        out_shape=[jax.ShapeDtypeStruct((k * CBLK, WIDE), bf16) for k in sizes],
        compiler_params=pltpu.CompilerParams(vmem_limit_bytes=48 * 2**20),
        cost_estimate=pl.CostEstimate(
            flops=84000000 * total, bytes_accessed=900000 * total, transcendentals=0
        ),
    )(places, own, other, feet)


def filter_kernel(bw, x, prec, out, pad, acc):
    nz, rows, _ = x.shape
    nb = 2 * nz
    per = rows // GROUP
    y, xx, z, c = (lax.axis_index(name) for name in AXES)
    base = (((y * SIDE + xx) * 2 + c) * nz + z) * per
    pad[:BMAX] = jnp.zeros((BMAX, rows, FR), bf16)
    pad[BMAX + nb :] = jnp.zeros((BMAX, rows, FR), bf16)
    for i in range(nz):
        pad[BMAX + 2 * i + c] = x[i, :, :FR]
        pad[BMAX + 2 * i + 1 - c] = x[i, :, FR:]
    reach = jnp.concatenate(
        [jnp.full((1, GROUP, FR), bw[base + g], jnp.int32) for g in range(per)], axis=1
    )
    for d in range(-BMAX, BMAX + 1):
        src = pad[BMAX + d : BMAX + d + nb].reshape(nb * rows, FR)
        term = jnp.dot(src, prec[d + BMAX], preferred_element_type=f32).reshape(nb, rows, FR)
        term = jnp.where(reach >= abs(d), term, 0.0)
        if d == -BMAX:
            acc[...] = term
        else:
            acc[...] += term
    for i in range(nz):
        out[i, :, :FR] = acc[2 * i + c].astype(bf16)
        out[i, :, FR:] = acc[2 * i + 1 - c].astype(bf16)


def band_filter(x, bw, prec):
    nz, rows, _ = x.shape
    vmem = pl.BlockSpec(memory_space=pltpu.VMEM)
    return pl.pallas_call(
        filter_kernel,
        in_specs=[pl.BlockSpec(memory_space=pltpu.SMEM), vmem, vmem],
        out_specs=vmem,
        out_shape=jax.ShapeDtypeStruct(x.shape, bf16),
        scratch_shapes=[
            pltpu.VMEM((2 * nz + 2 * BMAX, rows, FR), bf16),
            pltpu.VMEM((2 * nz, rows, FR), f32),
        ],
        cost_estimate=pl.CostEstimate(flops=369000000, bytes_accessed=800000, transcendentals=0),
    )(bw, x, prec)


def rebuild_kernel(places, movie, feet, *rest):
    parts = rest[:-9]
    keep, send, buf, sems, slot_of, place_of, held, part_sems, acc = rest[-9:]
    copies, at = [], 0
    for k, part in enumerate(parts):
        rows = part.shape[0]
        copies.append(pltpu.make_async_copy(part, held.at[pl.ds(at, rows)], part_sems.at[k]))
        at += rows
    for copy in copies:
        copy.start()
    count = start_slots(places, feet, buf, sems, slot_of, place_of, 0, OWNED)
    tiles = movie.shape[0]
    for k in range(UNROLL - 1):
        slot_of[count + k] = tiles * SLOTS
        place_of[count + k] = 0
    acc[...] = jnp.zeros_like(acc)
    for copy in copies:
        copy.wait()

    def some(g, carry):
        j = g * UNROLL
        wait_slots(j, count, feet, buf, sems, slot_of)
        for k in range(UNROLL):
            rows = pl.ds(pl.multiple_of(place_of[j + k] * CBLK, CBLK), CBLK)
            acc[slot_of[j + k] // SLOTS] += jnp.dot(
                buf[j + k], held[rows, :], preferred_element_type=f32
            )
        return carry

    lax.fori_loop(0, (count + UNROLL - 1) // UNROLL, some, 0)
    keep[...] = movie[...].astype(f32) - acc[:tiles, :, :FR]
    send[...] = acc[:tiles, :, FR:].astype(bf16)


def rebuild(movie, feet, places, parts):
    tiles = movie.shape[0]
    slots = places.shape[0]
    room = slots + UNROLL - 1
    vmem = pl.BlockSpec(memory_space=pltpu.VMEM)
    hbm = pl.BlockSpec(memory_space=pl.ANY)
    return pl.pallas_call(
        rebuild_kernel,
        in_specs=[pl.BlockSpec(memory_space=pltpu.SMEM), vmem, hbm] + [hbm] * len(parts),
        out_specs=[vmem, vmem],
        scratch_shapes=[
            pltpu.VMEM((room, TILE, CBLK), bf16),
            pltpu.SemaphoreType.DMA((slots,)),
            pltpu.SMEM((room,), jnp.int32),
            pltpu.SMEM((room,), jnp.int32),
            pltpu.VMEM((OWNED * CBLK, WIDE), bf16),
            pltpu.SemaphoreType.DMA((len(parts),)),
            pltpu.VMEM((tiles + 1, TILE, WIDE), f32),
        ],
        out_shape=[
            jax.ShapeDtypeStruct(movie.shape, f32),
            jax.ShapeDtypeStruct(movie.shape, bf16),
        ],
        compiler_params=pltpu.CompilerParams(vmem_limit_bytes=48 * 2**20),
        cost_estimate=pl.CostEstimate(flops=1342177280, bytes_accessed=12000000, transcendentals=0),
    )(places, movie, feet, *parts)


def shift(v, first, k):
    nz = lax.axis_size("z")
    pairs = []
    for y in range(SIDE):
        for x in range(SIDE):
            for z in range(nz):
                for c in range(2):
                    along_y = (c == 0) == first
                    ty, tx = ((y + k) % SIDE, x) if along_y else (y, (x + k) % SIDE)
                    pairs.append(
                        (((y * SIDE + x) * nz + z) * 2 + c, ((ty * SIDE + tx) * nz + z) * 2 + c)
                    )
    return lax.ppermute(v, AXES, pairs)


def swap(v):
    return lax.ppermute(v, "c", [(0, 1), (1, 0)])


def add(*terms):
    total = terms[0].astype(f32)
    for term in terms[1:]:
        total = total + term.astype(f32)
    return total.astype(bf16)


def reduce_long(own, up_lo, up_hi, down_lo, down_hi, far_lo, far_hi, first):
    far_up = shift(far_lo, first, 1)
    far_down = shift(far_hi, first, -1)
    got_hi = shift(up_hi, first, 1)
    got_lo = shift(down_lo, first, -1)
    late_lo = shift(add(up_lo, far_up), first, 1)
    late_hi = shift(add(down_hi, far_down), first, -1)
    h = own.shape[0] // 2
    return add(own[:h], got_lo, late_lo), add(own[h:], got_hi, late_hi)


def reduce_short(own, up, down, far, first):
    h = far.shape[0] // 2
    far_up = shift(far[:h], first, 1)
    far_down = shift(far[h:], first, -1)
    got_up = shift(jnp.concatenate([add(up[:h], far_up), up[h:]], axis=0), first, 1)
    got_down = shift(jnp.concatenate([down[:h], add(down[h:], far_down)], axis=0), first, -1)
    return add(own, got_up, got_down)


def gather_ring(v, first):
    h = v.shape[0] // 2
    up, down = shift(v, first, -1), shift(v, first, 1)
    far_lo, far_hi = shift(down[:h], first, 1), shift(up[h:], first, -1)
    return v, up, down, far_lo, far_hi


def shards(movie, noise_weight, footprints, block_ids, band_width, precision_blocks):
    nz = lax.axis_size("z")
    c = lax.axis_index("c")
    tiles = movie.shape[0]
    places = places_of(block_ids)
    feet = footprints.reshape(tiles * SLOTS, TILE, CBLK)
    weighted = (noise_weight[:, :, None] * movie.astype(f32)).astype(bf16)
    other = swap(weighted)
    far_lo, far_hi = project(weighted, other, feet, places, 12, (2, 2))
    pieces = project(weighted, other, feet, places, 0, (4, 2, 2, 2, 2))
    lo, hi = reduce_long(*pieces, far_lo, far_hi, True)
    projected = reduce_short(lo[:CBLK], lo[CBLK:], hi[:CBLK], hi[CBLK:], False)
    regrouped = lax.all_to_all(projected.reshape(nz, CBLK // nz, WIDE), "z", 0, 0, tiled=True)
    filtered = band_filter(regrouped, band_width, precision_blocks)
    back = lax.all_to_all(filtered, "z", 0, 0, tiled=True).reshape(CBLK, WIDE)
    row = jnp.concatenate(gather_ring(back, False), axis=0)
    parts = gather_ring(row, True)
    mine, theirs = back[:, :FR], swap(back[:, FR:])
    traces = jnp.where(
        c == 0, jnp.concatenate([mine, theirs], 0), jnp.concatenate([theirs, mine], 0)
    )
    keep, send = rebuild(movie, feet, places, parts)
    residual = (keep - swap(send).astype(f32)).astype(bf16)
    return traces, residual


def solution(mesh):
    devices = mesh.devices.reshape(SIDE, SIDE, mesh.devices.shape[1] // 2, 2)
    grid = Mesh(devices, AXES)
    pix, tm = ("y", "x"), ("z", "c")
    return jax.shard_map(
        shards,
        mesh=grid,
        in_specs=(
            P(pix, None, tm),
            P(pix, None),
            P(pix, None, None, None),
            P(pix, None),
            P(),
            P(),
        ),
        out_specs=(P(pix, tm), P(pix, None, tm)),
        check_vma=False,
    )
```

```python
import functools

import jax
import jax.numpy as jnp
from jax import lax
from jax.experimental import pallas as pl
from jax.experimental.pallas import tpu as pltpu
from jax.sharding import Mesh
from jax.sharding import PartitionSpec as P

CBLK = 512
TILE = 128
SLOTS = 4
GROUP = 16
BMAX = 5
FR = 128
WIDE = 2 * FR
SIDE = 4
OWNED = SIDE * SIDE
f32 = jnp.float32
bf16 = jnp.bfloat16
UNROLL = 4
AXES = ("y", "x", "z", "c")


def near(target, here):
    d = (target - here) & 3
    return d ^ (d >> 1)


def places_of(block_ids):
    y, x, c = lax.axis_index("y"), lax.axis_index("x"), lax.axis_index("c")
    owner = block_ids >> 1
    ny, nx = near(owner >> 2, y), near(owner & 3, x)
    at = jnp.where(c == 0, ny * 4 + nx, nx * 4 + ny)
    at = jnp.where((block_ids & 1) == c, at, -1).reshape(-1)
    row, column = at >> 2, at & 3
    near_rows = (at >= 0) & (row < 3)
    far_row = jnp.where(row == 3, column, -1)
    soon = jnp.where(near_rows & (column == 3), 4 + row, far_row)
    others = jnp.where(near_rows & (column < 3), row * 3 + column, -1)
    return far_row, soon, others, jnp.where(near_rows, at, -1)


def list_slots(places, slot_of, place_of, spare_slot, spare_place, visit=None):
    def scan(i, count):
        at = places[i]
        slot_of[count] = i
        place_of[count] = at
        if visit is not None:
            pl.when(at >= 0)(lambda: visit(i, count))
        return count + (at >= 0).astype(jnp.int32)

    count = lax.fori_loop(0, places.shape[0], scan, 0, unroll=4)
    for k in range(UNROLL - 1):
        slot_of[count + k] = spare_slot
        place_of[count + k] = spare_place
    return count


def project_kernel(places, own, other, feet, *rest):
    outs = rest[:-5]
    slot_of, place_of, acc, buf, sems = rest[-5:]

    def copy(i, j):
        return pltpu.make_async_copy(feet.at[i], buf.at[j], sems.at[j])

    count = list_slots(
        places, slot_of, place_of, 0, acc.shape[0] - 1, lambda i, j: copy(i, j).start()
    )
    acc[...] = jnp.zeros_like(acc)

    def some(g, carry):
        for k in range(UNROLL):
            j = g * UNROLL + k
            pl.when(j < count)(lambda j=j: copy(slot_of[j], j).wait())
        for k in range(UNROLL):
            j = g * UNROLL + k
            i = slot_of[j]
            w = jnp.concatenate([own[i // SLOTS], other[i // SLOTS]], axis=1)
            acc[place_of[j]] += lax.dot_general(
                buf[j], w, (((0,), (0,)), ((), ())), preferred_element_type=f32
            )
        return carry

    lax.fori_loop(0, (count + UNROLL - 1) // UNROLL, some, 0)
    at = 0
    for out in outs:
        k = out.shape[0] // CBLK
        out[...] = acc[at : at + k].reshape(out.shape).astype(bf16)
        at += k


def project(own, other, feet, places, sizes):
    slots = places.shape[0]
    room = slots + UNROLL
    total = sum(sizes)
    vmem = pl.BlockSpec(memory_space=pltpu.VMEM)
    hbm = pl.BlockSpec(memory_space=pltpu.HBM)
    return pl.pallas_call(
        project_kernel,
        in_specs=[pl.BlockSpec(memory_space=pltpu.SMEM), vmem, vmem, hbm],
        out_specs=[vmem] * len(sizes),
        scratch_shapes=[
            pltpu.SMEM((room,), jnp.int32),
            pltpu.SMEM((room,), jnp.int32),
            pltpu.VMEM((total + 1, CBLK, WIDE), f32),
            pltpu.VMEM((room, TILE, CBLK), bf16),
            pltpu.SemaphoreType.DMA((slots,)),
        ],
        out_shape=[jax.ShapeDtypeStruct((k * CBLK, WIDE), bf16) for k in sizes],
        compiler_params=pltpu.CompilerParams(vmem_limit_bytes=48 * 2**20),
        cost_estimate=pl.CostEstimate(
            flops=84000000 * total, bytes_accessed=900000 * total, transcendentals=0
        ),
    )(places, own, other, feet)


def filter_kernel(bw, x, prec, out, pad, acc):
    nz, rows, _ = x.shape
    nb = 2 * nz
    per = rows // GROUP
    y, xx, z, c = (lax.axis_index(name) for name in AXES)
    base = (((y * SIDE + xx) * 2 + c) * nz + z) * per
    pad[:BMAX] = jnp.zeros((BMAX, rows, FR), bf16)
    pad[BMAX + nb :] = jnp.zeros((BMAX, rows, FR), bf16)
    for i in range(nz):
        pad[BMAX + 2 * i + c] = x[i, :, :FR]
        pad[BMAX + 2 * i + 1 - c] = x[i, :, FR:]
    reach = jnp.concatenate(
        [jnp.full((1, GROUP, FR), bw[base + g], jnp.int32) for g in range(per)], axis=1
    )
    for d in range(-BMAX, BMAX + 1):
        src = pad[BMAX + d : BMAX + d + nb].reshape(nb * rows, FR)
        term = jnp.dot(src, prec[d + BMAX], preferred_element_type=f32).reshape(nb, rows, FR)
        term = jnp.where(reach >= abs(d), term, 0.0)
        if d == -BMAX:
            acc[...] = term
        else:
            acc[...] += term
    for i in range(nz):
        out[i, :, :FR] = acc[2 * i + c].astype(bf16)
        out[i, :, FR:] = acc[2 * i + 1 - c].astype(bf16)


def band_filter(x, bw, prec):
    nz, rows, _ = x.shape
    vmem = pl.BlockSpec(memory_space=pltpu.VMEM)
    return pl.pallas_call(
        filter_kernel,
        in_specs=[pl.BlockSpec(memory_space=pltpu.SMEM), vmem, vmem],
        out_specs=vmem,
        out_shape=jax.ShapeDtypeStruct(x.shape, bf16),
        scratch_shapes=[
            pltpu.VMEM((2 * nz + 2 * BMAX, rows, FR), bf16),
            pltpu.VMEM((2 * nz, rows, FR), f32),
        ],
        cost_estimate=pl.CostEstimate(flops=369000000, bytes_accessed=800000, transcendentals=0),
    )(bw, x, prec)


def rebuild_kernel(places, feet, *rest, moves, last):
    parts, rest = rest[: len(moves)], rest[len(moves) :]
    slot_of, place_of, held, acc = rest[-4:]
    tiles = acc.shape[0] - 1
    count = list_slots(places, slot_of, place_of, tiles * SLOTS, 0)
    for part, cuts in zip(parts, moves):
        for src, rows, dst in cuts:
            held[dst : dst + rows] = part[src : src + rows]
    if last:
        movie, before, keep, send = rest[:4]
        acc[:tiles] = before[...]
    else:
        acc[...] = jnp.zeros_like(acc)

    def some(g, carry):
        for k in range(UNROLL):
            j = g * UNROLL + k
            i = slot_of[j]
            rows = pl.ds(pl.multiple_of(place_of[j] * CBLK, CBLK), CBLK)
            acc[i // SLOTS] += jnp.dot(
                feet[jnp.minimum(i, tiles * SLOTS - 1)],
                held[rows, :],
                preferred_element_type=f32,
            )
        return carry

    lax.fori_loop(0, (count + UNROLL - 1) // UNROLL, some, 0)
    if last:
        keep[...] = movie[...].astype(f32) - acc[:tiles, :, :FR]
        send[...] = acc[:tiles, :, FR:].astype(bf16)
    else:
        rest[0][...] = acc[:tiles]


def rebuild(feet, places, parts, moves, blocks, extra=()):
    slots = places.shape[0]
    tiles = slots // SLOTS
    room = slots + UNROLL
    vmem = pl.BlockSpec(memory_space=pltpu.VMEM)
    if extra:
        outs = [
            jax.ShapeDtypeStruct((tiles, TILE, FR), f32),
            jax.ShapeDtypeStruct((tiles, TILE, FR), bf16),
        ]
    else:
        outs = [jax.ShapeDtypeStruct((tiles, TILE, WIDE), f32)]
    return pl.pallas_call(
        functools.partial(rebuild_kernel, moves=moves, last=bool(extra)),
        in_specs=[pl.BlockSpec(memory_space=pltpu.SMEM)] + [vmem] * (1 + len(parts) + len(extra)),
        out_specs=[vmem] * len(outs),
        scratch_shapes=[
            pltpu.SMEM((room,), jnp.int32),
            pltpu.SMEM((room,), jnp.int32),
            pltpu.VMEM((blocks * CBLK, WIDE), bf16),
            pltpu.VMEM((tiles + 1, TILE, WIDE), f32),
        ],
        out_shape=outs,
        compiler_params=pltpu.CompilerParams(vmem_limit_bytes=30 * 2**20),
        cost_estimate=pl.CostEstimate(
            flops=84000000 * blocks, bytes_accessed=900000 * blocks, transcendentals=0
        ),
    )(places, feet, *parts, *extra)


def finish_kernel(keep, got, out):
    out[...] = (keep[...] - got[...].astype(f32)).astype(bf16)


def finish(keep, got):
    vmem = pl.BlockSpec(memory_space=pltpu.VMEM)
    return pl.pallas_call(
        finish_kernel,
        in_specs=[vmem, vmem],
        out_specs=vmem,
        out_shape=jax.ShapeDtypeStruct(got.shape, bf16),
    )(keep, got)


def shift(v, first, k):
    nz = lax.axis_size("z")
    pairs = []
    for y in range(SIDE):
        for x in range(SIDE):
            for z in range(nz):
                for c in range(2):
                    along_y = (c == 0) == first
                    ty, tx = ((y + k) % SIDE, x) if along_y else (y, (x + k) % SIDE)
                    pairs.append(
                        (((y * SIDE + x) * nz + z) * 2 + c, ((ty * SIDE + tx) * nz + z) * 2 + c)
                    )
    return lax.ppermute(v, AXES, pairs)


def swap(v):
    return lax.ppermute(v, "c", [(0, 1), (1, 0)])


def add(*terms):
    total = terms[0].astype(f32)
    for term in terms[1:]:
        total = total + term.astype(f32)
    return total.astype(bf16)


def reduce_short(own, up, down, far, first):
    h = far.shape[0] // 2
    far_up = shift(far[:h], first, 1)
    far_down = shift(far[h:], first, -1)
    got_up = shift(jnp.concatenate([add(up[:h], far_up), up[h:]], axis=0), first, 1)
    got_down = shift(jnp.concatenate([down[:h], add(down[h:], far_down)], axis=0), first, -1)
    return add(own, got_up, got_down)


def reduce_plane(weighted, other, feet, soon, others):
    far_lo, far_hi, own_far, up_far, down_far = project(
        weighted, other, feet, soon, (2, 2, 1, 1, 1)
    )
    far_up = shift(far_lo, True, 1)
    far_down = shift(far_hi, True, -1)
    got_up_far = shift(up_far, True, 1)
    got_down_far = shift(add(down_far, far_down[CBLK:]), True, -1)
    own, up_lo, up_mid, down_lo, down_mid = project(
        weighted, other, feet, others, (3, 2, 1, 2, 1)
    )
    up_lo, down_lo, got_up_far, got_down_far = lax.optimization_barrier(
        (up_lo, down_lo, got_up_far, got_down_far)
    )
    far = add(own_far, got_up_far, got_down_far)
    got_up = shift(jnp.concatenate([add(up_lo, far_up), up_mid], axis=0), True, 1)
    got_down = shift(
        jnp.concatenate([down_lo, add(down_mid, far_down[:CBLK])], axis=0), True, -1
    )
    near_rows = add(own, got_up, got_down)
    return reduce_short(
        near_rows[:CBLK], near_rows[CBLK : 2 * CBLK], near_rows[2 * CBLK :], far, False
    )


def row_moves(base):
    h = CBLK // 2
    return [
        [(0, CBLK, base)],
        [
            (0, CBLK, base + CBLK),
            (CBLK, h, base + 3 * CBLK),
            (CBLK + h, CBLK, base + 2 * CBLK),
            (2 * CBLK + h, h, base + 3 * CBLK + h),
        ],
    ]


def gather_plane(own):
    h = CBLK // 2
    up, down = shift(own, False, -1), shift(own, False, 1)
    up_own, down_own = shift(own, True, -1), shift(own, True, 1)
    far_lo, far_hi = shift(down[:h], False, 1), shift(up[h:], False, -1)
    others = jnp.concatenate([up, far_lo, down, far_hi], axis=0)
    others, up_own, down_own = lax.optimization_barrier((others, up_own, down_own))
    up_others, down_others = shift(others, True, -1), shift(others, True, 1)
    row = 4 * CBLK
    near_moves = row_moves(0) + row_moves(row) + row_moves(2 * row)
    m = CBLK + h
    far_own_lo, far_own_hi = shift(down_own[:h], True, 1), shift(up_own[h:], True, -1)
    up_others, down_others, far_own_lo, far_own_hi = lax.optimization_barrier(
        (up_others, down_others, far_own_lo, far_own_hi)
    )
    near_parts = (own, others, up_own, up_others, down_own, down_others)
    far_parts = (
        far_own_lo,
        far_own_hi,
        shift(down_others[:m], True, 1),
        shift(up_others[m:], True, -1),
    )
    far_moves = [
        [(0, h, 0)],
        [(0, h, h)],
        [(0, CBLK, CBLK), (CBLK, h, 3 * CBLK)],
        [(0, CBLK, 2 * CBLK), (CBLK, h, 3 * CBLK + h)],
    ]
    return near_parts, near_moves, far_parts, far_moves


def shards(movie, noise_weight, footprints, block_ids, band_width, precision_blocks):
    nz = lax.axis_size("z")
    c = lax.axis_index("c")
    tiles = movie.shape[0]
    far_row, soon, others, near_rows = places_of(block_ids)
    feet = footprints.reshape(tiles * SLOTS, TILE, CBLK)
    weighted = (noise_weight[:, :, None] * movie.astype(f32)).astype(bf16)
    projected = reduce_plane(
        weighted, swap(weighted), feet, soon, others
    )
    regrouped = lax.all_to_all(projected.reshape(nz, CBLK // nz, WIDE), "z", 0, 0, tiled=True)
    filtered = band_filter(regrouped, band_width, precision_blocks)
    back = lax.all_to_all(filtered, "z", 0, 0, tiled=True).reshape(CBLK, WIDE)
    near_parts, near_moves, far_parts, far_moves = gather_plane(back)
    mine, theirs = back[:, :FR], swap(back[:, FR:])
    traces = jnp.where(
        c == 0, jnp.concatenate([mine, theirs], 0), jnp.concatenate([theirs, mine], 0)
    )
    near_rows, traces = lax.optimization_barrier((near_rows, traces))
    (before,) = rebuild(feet, near_rows, near_parts, near_moves, 12)
    keep, send = rebuild(feet, far_row, far_parts, far_moves, 4, (movie, before))
    residual = finish(keep, swap(send))
    return traces, residual


def solution(mesh):
    devices = mesh.devices.reshape(SIDE, SIDE, mesh.devices.shape[1] // 2, 2)
    grid = Mesh(devices, AXES)
    pix, tm = ("y", "x"), ("z", "c")
    return jax.shard_map(
        shards,
        mesh=grid,
        in_specs=(
            P(pix, None, tm),
            P(pix, None),
            P(pix, None, None, None),
            P(pix, None),
            P(),
            P(),
        ),
        out_specs=(P(pix, tm), P(pix, None, tm)),
        check_vma=False,
    )
```

```python
import functools

import jax
import jax.numpy as jnp
from jax import lax
from jax.experimental import pallas as pl
from jax.experimental.pallas import tpu as pltpu
from jax.sharding import Mesh
from jax.sharding import PartitionSpec as P

CBLK = 512
TILE = 128
SLOTS = 4
GROUP = 16
BMAX = 5
FR = 128
WIDE = 2 * FR
SIDE = 4
OWNED = SIDE * SIDE
f32 = jnp.float32
bf16 = jnp.bfloat16
UNROLL = 4
AXES = ("y", "x", "z", "c")


def near(target, here):
    d = (target - here) & 3
    return d ^ (d >> 1)


def places_of(block_ids):
    y, x, c = lax.axis_index("y"), lax.axis_index("x"), lax.axis_index("c")
    owner = block_ids >> 1
    ny, nx = near(owner >> 2, y), near(owner & 3, x)
    at = jnp.where(c == 0, ny * 4 + nx, nx * 4 + ny)
    at = jnp.where((block_ids & 1) == c, at, -1).reshape(-1)
    row, column = at >> 2, at & 3
    near_rows = (at >= 0) & (row < 3)
    far_row = jnp.where(row == 3, column, -1)
    soon = jnp.where(near_rows & (column == 3), 4 + row, far_row)
    others = jnp.where(near_rows & (column < 3), row * 3 + column, -1)
    return far_row, soon, others, jnp.where(near_rows, at, -1)


def start_slots(places, feet, buf, sems, slot_of, place_of, spare_slot, spare_place):
    def scan(i, count):
        at = places[i]
        slot_of[count] = i
        place_of[count] = at

        @pl.when(at >= 0)
        def _():
            pltpu.make_async_copy(feet.at[i], buf.at[count], sems.at[count]).start()

        return count + (at >= 0).astype(jnp.int32)

    count = lax.fori_loop(0, places.shape[0], scan, 0, unroll=4)
    for k in range(UNROLL - 1):
        slot_of[count + k] = spare_slot
        place_of[count + k] = spare_place
    return count


def wait_slots(g, count, feet, buf, sems, slot_of):
    for k in range(UNROLL):
        j = g * UNROLL + k

        @pl.when(j < count)
        def _():
            pltpu.make_async_copy(feet.at[slot_of[j]], buf.at[j], sems.at[j]).wait()


def project_kernel(places, own, other, feet, *rest):
    outs = rest[:-5]
    slot_of, place_of, acc, buf, sems = rest[-5:]

    count = start_slots(places, feet, buf, sems, slot_of, place_of, 0, acc.shape[0] - 1)
    acc[...] = jnp.zeros_like(acc)

    def some(g, carry):
        wait_slots(g, count, feet, buf, sems, slot_of)
        for k in range(UNROLL):
            j = g * UNROLL + k
            i = slot_of[j]
            w = jnp.concatenate([own[i // SLOTS], other[i // SLOTS]], axis=1)
            acc[place_of[j]] += lax.dot_general(
                buf[j], w, (((0,), (0,)), ((), ())), preferred_element_type=f32
            )
        return carry

    lax.fori_loop(0, (count + UNROLL - 1) // UNROLL, some, 0)
    at = 0
    for out in outs:
        k = out.shape[0] // CBLK
        out[...] = acc[at : at + k].reshape(out.shape).astype(bf16)
        at += k


def project(own, other, feet, places, sizes):
    slots = places.shape[0]
    room = slots + UNROLL
    total = sum(sizes)
    vmem = pl.BlockSpec(memory_space=pltpu.VMEM)
    hbm = pl.BlockSpec(memory_space=pltpu.HBM)
    return pl.pallas_call(
        project_kernel,
        in_specs=[pl.BlockSpec(memory_space=pltpu.SMEM), vmem, vmem, hbm],
        out_specs=[vmem] * len(sizes),
        scratch_shapes=[
            pltpu.SMEM((room,), jnp.int32),
            pltpu.SMEM((room,), jnp.int32),
            pltpu.VMEM((total + 1, CBLK, WIDE), f32),
            pltpu.VMEM((room, TILE, CBLK), bf16),
            pltpu.SemaphoreType.DMA((slots,)),
        ],
        out_shape=[jax.ShapeDtypeStruct((k * CBLK, WIDE), bf16) for k in sizes],
        compiler_params=pltpu.CompilerParams(vmem_limit_bytes=45 * 2**20),
        cost_estimate=pl.CostEstimate(
            flops=84000000 * total, bytes_accessed=900000 * total, transcendentals=0
        ),
    )(places, own, other, feet)


def filter_kernel(bw, x, prec, out, pad, acc):
    nz, rows, _ = x.shape
    nb = 2 * nz
    per = rows // GROUP
    y, xx, z, c = (lax.axis_index(name) for name in AXES)
    base = (((y * SIDE + xx) * 2 + c) * nz + z) * per
    pad[:BMAX] = jnp.zeros((BMAX, rows, FR), bf16)
    pad[BMAX + nb :] = jnp.zeros((BMAX, rows, FR), bf16)
    for i in range(nz):
        pad[BMAX + 2 * i + c] = x[i, :, :FR]
        pad[BMAX + 2 * i + 1 - c] = x[i, :, FR:]
    reach = jnp.concatenate(
        [jnp.full((1, GROUP, FR), bw[base + g], jnp.int32) for g in range(per)], axis=1
    )
    for d in range(-BMAX, BMAX + 1):
        src = pad[BMAX + d : BMAX + d + nb].reshape(nb * rows, FR)
        term = jnp.dot(src, prec[d + BMAX], preferred_element_type=f32).reshape(nb, rows, FR)
        term = jnp.where(reach >= abs(d), term, 0.0)
        if d == -BMAX:
            acc[...] = term
        else:
            acc[...] += term
    for i in range(nz):
        out[i, :, :FR] = acc[2 * i + c].astype(bf16)
        out[i, :, FR:] = acc[2 * i + 1 - c].astype(bf16)


def band_filter(x, bw, prec):
    nz, rows, _ = x.shape
    vmem = pl.BlockSpec(memory_space=pltpu.VMEM)
    return pl.pallas_call(
        filter_kernel,
        in_specs=[pl.BlockSpec(memory_space=pltpu.SMEM), vmem, vmem],
        out_specs=vmem,
        out_shape=jax.ShapeDtypeStruct(x.shape, bf16),
        scratch_shapes=[
            pltpu.VMEM((2 * nz + 2 * BMAX, rows, FR), bf16),
            pltpu.VMEM((2 * nz, rows, FR), f32),
        ],
        compiler_params=pltpu.CompilerParams(vmem_limit_bytes=8 * 2**20),
        cost_estimate=pl.CostEstimate(flops=369000000, bytes_accessed=800000, transcendentals=0),
    )(bw, x, prec)


def rebuild_kernel(places, feet, *rest, moves, last):
    parts, rest = rest[: len(moves)], rest[len(moves) :]
    slot_of, place_of, held, acc, buf, sems = rest[-6:]
    tiles = acc.shape[0] - 1
    count = start_slots(places, feet, buf, sems, slot_of, place_of, tiles * SLOTS, 0)
    for part, cuts in zip(parts, moves):
        for src, rows, dst in cuts:
            held[dst : dst + rows] = part[src : src + rows]
    if last:
        movie, before, keep, send = rest[:4]
        acc[:tiles] = before[...]
    else:
        acc[...] = jnp.zeros_like(acc)

    def some(g, carry):
        wait_slots(g, count, feet, buf, sems, slot_of)
        for k in range(UNROLL):
            j = g * UNROLL + k
            rows = pl.ds(pl.multiple_of(place_of[j] * CBLK, CBLK), CBLK)
            acc[slot_of[j] // SLOTS] += jnp.dot(
                buf[j], held[rows, :], preferred_element_type=f32
            )
        return carry

    lax.fori_loop(0, (count + UNROLL - 1) // UNROLL, some, 0)
    if last:
        keep[...] = movie[...].astype(f32) - acc[:tiles, :, :FR]
        send[...] = acc[:tiles, :, FR:].astype(bf16)
    else:
        rest[0][...] = acc[:tiles]


def rebuild(feet, places, parts, moves, blocks, extra=()):
    slots = places.shape[0]
    tiles = slots // SLOTS
    room = slots + UNROLL
    vmem = pl.BlockSpec(memory_space=pltpu.VMEM)
    if extra:
        outs = [
            jax.ShapeDtypeStruct((tiles, TILE, FR), f32),
            jax.ShapeDtypeStruct((tiles, TILE, FR), bf16),
        ]
    else:
        outs = [jax.ShapeDtypeStruct((tiles, TILE, WIDE), f32)]
    return pl.pallas_call(
        functools.partial(rebuild_kernel, moves=moves, last=bool(extra)),
        in_specs=[
            pl.BlockSpec(memory_space=pltpu.SMEM),
            pl.BlockSpec(memory_space=pltpu.HBM),
        ]
        + [vmem] * (len(parts) + len(extra)),
        out_specs=[vmem] * len(outs),
        scratch_shapes=[
            pltpu.SMEM((room,), jnp.int32),
            pltpu.SMEM((room,), jnp.int32),
            pltpu.VMEM((blocks * CBLK, WIDE), bf16),
            pltpu.VMEM((tiles + 1, TILE, WIDE), f32),
            pltpu.VMEM((room, TILE, CBLK), bf16),
            pltpu.SemaphoreType.DMA((slots,)),
        ],
        out_shape=outs,
        compiler_params=pltpu.CompilerParams(vmem_limit_bytes=45 * 2**20),
        cost_estimate=pl.CostEstimate(
            flops=84000000 * blocks, bytes_accessed=900000 * blocks, transcendentals=0
        ),
    )(places, feet, *parts, *extra)


def finish_kernel(keep, got, out):
    out[...] = (keep[...] - got[...].astype(f32)).astype(bf16)


def finish(keep, got):
    vmem = pl.BlockSpec(memory_space=pltpu.VMEM)
    return pl.pallas_call(
        finish_kernel,
        in_specs=[vmem, vmem],
        out_specs=vmem,
        out_shape=jax.ShapeDtypeStruct(got.shape, bf16),
        compiler_params=pltpu.CompilerParams(vmem_limit_bytes=8 * 2**20),
        cost_estimate=pl.CostEstimate(flops=700000, bytes_accessed=2600000, transcendentals=0),
    )(keep, got)


def shift(v, first, k):
    nz = lax.axis_size("z")
    pairs = []
    for y in range(SIDE):
        for x in range(SIDE):
            for z in range(nz):
                for c in range(2):
                    along_y = (c == 0) == first
                    ty, tx = ((y + k) % SIDE, x) if along_y else (y, (x + k) % SIDE)
                    pairs.append(
                        (((y * SIDE + x) * nz + z) * 2 + c, ((ty * SIDE + tx) * nz + z) * 2 + c)
                    )
    return lax.ppermute(v, AXES, pairs)


def swap(v):
    return lax.ppermute(v, "c", [(0, 1), (1, 0)])


def add(*terms):
    total = terms[0].astype(f32)
    for term in terms[1:]:
        total = total + term.astype(f32)
    return total.astype(bf16)


def reduce_short(own, up, down, far, first):
    h = far.shape[0] // 2
    far_up = shift(far[:h], first, 1)
    far_down = shift(far[h:], first, -1)
    got_up = shift(jnp.concatenate([add(up[:h], far_up), up[h:]], axis=0), first, 1)
    got_down = shift(jnp.concatenate([down[:h], add(down[h:], far_down)], axis=0), first, -1)
    return add(own, got_up, got_down)


def reduce_plane(weighted, other, feet, soon, others):
    far_lo, far_hi, own_far, up_far, down_far = project(
        weighted, other, feet, soon, (2, 2, 1, 1, 1)
    )
    far_up = shift(far_lo, True, 1)
    far_down = shift(far_hi, True, -1)
    got_up_far = shift(up_far, True, 1)
    got_down_far = shift(add(down_far, far_down[CBLK:]), True, -1)
    own, up_lo, up_mid, down_lo, down_mid = project(
        weighted, other, feet, others, (3, 2, 1, 2, 1)
    )
    down_lo, got_up_far, got_down_far = lax.optimization_barrier(
        (down_lo, got_up_far, got_down_far)
    )
    far = add(own_far, got_up_far, got_down_far)
    got_up = shift(jnp.concatenate([add(up_lo, far_up), up_mid], axis=0), True, 1)
    got_down = shift(
        jnp.concatenate([down_lo, add(down_mid, far_down[:CBLK])], axis=0), True, -1
    )
    near_rows = add(own, got_up, got_down)
    return reduce_short(
        near_rows[:CBLK], near_rows[CBLK : 2 * CBLK], near_rows[2 * CBLK :], far, False
    )


def row_moves(base):
    h = CBLK // 2
    return [
        [(0, CBLK, base)],
        [
            (0, CBLK, base + CBLK),
            (CBLK, h, base + 3 * CBLK),
            (CBLK + h, CBLK, base + 2 * CBLK),
            (2 * CBLK + h, h, base + 3 * CBLK + h),
        ],
    ]


def gather_plane(own):
    h = CBLK // 2
    up, down = shift(own, False, -1), shift(own, False, 1)
    up_own, down_own = shift(own, True, -1), shift(own, True, 1)
    up, down, up_own, down_own = lax.optimization_barrier((up, down, up_own, down_own))
    far_lo, far_hi = shift(down[:h], False, 1), shift(up[h:], False, -1)
    others = jnp.concatenate([up, far_lo, down, far_hi], axis=0)
    up_others, down_others = shift(others, True, -1), shift(others, True, 1)
    row = 4 * CBLK
    near_parts = (own, others, up_own, up_others, down_own, down_others)
    near_moves = row_moves(0) + row_moves(row) + row_moves(2 * row)
    m = CBLK + h
    far_parts = (
        shift(jnp.concatenate([down_own[:h], down_others[:m]], axis=0), True, 1),
        shift(jnp.concatenate([up_own[h:], up_others[m:]], axis=0), True, -1),
    )
    far_moves = [
        [(0, h, 0), (h, CBLK, CBLK), (m, h, 3 * CBLK)],
        [(0, h, h), (h, CBLK, 2 * CBLK), (m, h, 3 * CBLK + h)],
    ]
    return near_parts, near_moves, far_parts, far_moves


def shards(movie, noise_weight, footprints, block_ids, band_width, precision_blocks):
    nz = lax.axis_size("z")
    c = lax.axis_index("c")
    tiles = movie.shape[0]
    far_row, soon, others, near_rows = places_of(block_ids)
    feet = footprints.reshape(tiles * SLOTS, TILE, CBLK)
    weighted = (noise_weight[:, :, None] * movie.astype(f32)).astype(bf16)
    projected = reduce_plane(
        weighted, swap(weighted), feet, soon, others
    )
    regrouped = lax.all_to_all(projected.reshape(nz, CBLK // nz, WIDE), "z", 0, 0, tiled=True)
    filtered = band_filter(regrouped, band_width, precision_blocks)
    back = lax.all_to_all(filtered, "z", 0, 0, tiled=True).reshape(CBLK, WIDE)
    near_parts, near_moves, far_parts, far_moves = gather_plane(back)
    mine, theirs = back[:, :FR], swap(back[:, FR:])
    traces = jnp.where(
        c == 0, jnp.concatenate([mine, theirs], 0), jnp.concatenate([theirs, mine], 0)
    )
    near_rows, traces = lax.optimization_barrier((near_rows, traces))
    (before,) = rebuild(feet, near_rows, near_parts, near_moves, 12)
    keep, send = rebuild(feet, far_row, far_parts, far_moves, 4, (movie, before))
    residual = finish(keep, swap(send))
    return traces, residual


def solution(mesh):
    devices = mesh.devices.reshape(SIDE, SIDE, mesh.devices.shape[1] // 2, 2)
    grid = Mesh(devices, AXES)
    pix, tm = ("y", "x"), ("z", "c")
    return jax.shard_map(
        shards,
        mesh=grid,
        in_specs=(
            P(pix, None, tm),
            P(pix, None),
            P(pix, None, None, None),
            P(pix, None),
            P(),
            P(),
        ),
        out_specs=(P(pix, tm), P(pix, None, tm)),
        check_vma=False,
    )
```

```python
import functools

import jax
import jax.numpy as jnp
from jax import lax
from jax.experimental import pallas as pl
from jax.experimental.pallas import tpu as pltpu
from jax.sharding import Mesh
from jax.sharding import PartitionSpec as P

CBLK = 512
TILE = 128
SLOTS = 4
GROUP = 16
BMAX = 5
FR = 128
WIDE = 2 * FR
SIDE = 4
OWNED = SIDE * SIDE
f32 = jnp.float32
bf16 = jnp.bfloat16
UNROLL = 4
AXES = ("y", "x", "z", "c")


def places_of(block_ids):
    y, x, c = lax.axis_index("y"), lax.axis_index("x"), lax.axis_index("c")
    owner = block_ids >> 1
    dy, dx = ((owner >> 2) - y) & 3, ((owner & 3) - x) & 3
    i, j = jnp.where(c == 0, dy, dx).reshape(-1), jnp.where(c == 0, dx, dy).reshape(-1)
    mine = ((block_ids & 1) == c).reshape(-1)
    ni, nj = i ^ (i >> 1), j ^ (j >> 1)

    def part(where, at):
        return jnp.where(mine & where, at, -1)

    far = i == 2
    soon = part(far | (j == 2), jnp.where(far, nj, 4 + ni))
    later = part(~far & (j != 2), ni * 3 + nj)
    first = part((i == 0) | (~far & (j == 0)), jnp.where(i == 0, j, 4 + (i >> 1)))
    second = part(jnp.where(far, j == 0, (i != 0) & (j != 0)), jnp.where(far, 6, (i >> 1) * 3 + j - 1))
    third = part(far & (j != 0), j - 1)
    return soon, later, first, second, third


def start_slots(places, feet, buf, sems, slot_of, place_of, spare_slot, spare_place):
    def scan(i, count):
        at = places[i]
        slot_of[count] = i
        place_of[count] = at

        @pl.when(at >= 0)
        def _():
            pltpu.make_async_copy(feet.at[i], buf.at[count], sems.at[count]).start()

        return count + (at >= 0).astype(jnp.int32)

    count = lax.fori_loop(0, places.shape[0], scan, 0, unroll=4)
    for k in range(UNROLL - 1):
        slot_of[count + k] = spare_slot
        place_of[count + k] = spare_place
    return count


def wait_slots(g, count, feet, buf, sems, slot_of):
    for k in range(UNROLL):
        j = g * UNROLL + k

        @pl.when(j < count)
        def _():
            pltpu.make_async_copy(feet.at[slot_of[j]], buf.at[j], sems.at[j]).wait()


def project_kernel(places, own, other, feet, *rest):
    outs = rest[:-5]
    slot_of, place_of, acc, buf, sems = rest[-5:]

    count = start_slots(places, feet, buf, sems, slot_of, place_of, 0, acc.shape[0] - 1)
    acc[...] = jnp.zeros_like(acc)

    def some(g, carry):
        wait_slots(g, count, feet, buf, sems, slot_of)
        for k in range(UNROLL):
            j = g * UNROLL + k
            i = slot_of[j]
            w = jnp.concatenate([own[i // SLOTS], other[i // SLOTS]], axis=1)
            acc[place_of[j]] += lax.dot_general(
                buf[j], w, (((0,), (0,)), ((), ())), preferred_element_type=f32
            )
        return carry

    lax.fori_loop(0, (count + UNROLL - 1) // UNROLL, some, 0)
    at = 0
    for out in outs:
        k = out.shape[0] // CBLK
        out[...] = acc[at : at + k].reshape(out.shape).astype(bf16)
        at += k


def project(own, other, feet, places, sizes):
    slots = places.shape[0]
    room = slots + UNROLL
    total = sum(sizes)
    vmem = pl.BlockSpec(memory_space=pltpu.VMEM)
    hbm = pl.BlockSpec(memory_space=pltpu.HBM)
    return pl.pallas_call(
        project_kernel,
        in_specs=[pl.BlockSpec(memory_space=pltpu.SMEM), vmem, vmem, hbm],
        out_specs=[vmem] * len(sizes),
        scratch_shapes=[
            pltpu.SMEM((room,), jnp.int32),
            pltpu.SMEM((room,), jnp.int32),
            pltpu.VMEM((total + 1, CBLK, WIDE), f32),
            pltpu.VMEM((room, TILE, CBLK), bf16),
            pltpu.SemaphoreType.DMA((slots,)),
        ],
        out_shape=[jax.ShapeDtypeStruct((k * CBLK, WIDE), bf16) for k in sizes],
        compiler_params=pltpu.CompilerParams(vmem_limit_bytes=45 * 2**20),
        cost_estimate=pl.CostEstimate(
            flops=84000000 * total, bytes_accessed=900000 * total, transcendentals=0
        ),
    )(places, own, other, feet)


def filter_kernel(bw, x, prec, out, pad, acc):
    nz, rows, _ = x.shape
    nb = 2 * nz
    per = rows // GROUP
    y, xx, z, c = (lax.axis_index(name) for name in AXES)
    base = (((y * SIDE + xx) * 2 + c) * nz + z) * per
    pad[:BMAX] = jnp.zeros((BMAX, rows, FR), bf16)
    pad[BMAX + nb :] = jnp.zeros((BMAX, rows, FR), bf16)
    for i in range(nz):
        pad[BMAX + 2 * i + c] = x[i, :, :FR]
        pad[BMAX + 2 * i + 1 - c] = x[i, :, FR:]
    reach = jnp.concatenate(
        [jnp.full((1, GROUP, FR), bw[base + g], jnp.int32) for g in range(per)], axis=1
    )
    for d in range(-BMAX, BMAX + 1):
        src = pad[BMAX + d : BMAX + d + nb].reshape(nb * rows, FR)
        term = jnp.dot(src, prec[d + BMAX], preferred_element_type=f32).reshape(nb, rows, FR)
        term = jnp.where(reach >= abs(d), term, 0.0)
        if d == -BMAX:
            acc[...] = term
        else:
            acc[...] += term
    for i in range(nz):
        out[i, :, :FR] = acc[2 * i + c].astype(bf16)
        out[i, :, FR:] = acc[2 * i + 1 - c].astype(bf16)


def band_filter(x, bw, prec):
    nz, rows, _ = x.shape
    vmem = pl.BlockSpec(memory_space=pltpu.VMEM)
    return pl.pallas_call(
        filter_kernel,
        in_specs=[pl.BlockSpec(memory_space=pltpu.SMEM), vmem, vmem],
        out_specs=vmem,
        out_shape=jax.ShapeDtypeStruct(x.shape, bf16),
        scratch_shapes=[
            pltpu.VMEM((2 * nz + 2 * BMAX, rows, FR), bf16),
            pltpu.VMEM((2 * nz, rows, FR), f32),
        ],
        compiler_params=pltpu.CompilerParams(vmem_limit_bytes=8 * 2**20),
        cost_estimate=pl.CostEstimate(flops=369000000, bytes_accessed=800000, transcendentals=0),
    )(bw, x, prec)


def rebuild_kernel(places, feet, *rest, n_parts, start, end):
    parts, rest = rest[:n_parts], rest[n_parts:]
    rest, (slot_of, place_of, held, buf, sems) = rest[:-5], rest[-5:]
    if end:
        movie, before, keep, send, acc = rest
    elif start:
        (acc,) = rest
    else:
        before, acc = rest
    tiles = acc.shape[0] - 1
    count = start_slots(places, feet, buf, sems, slot_of, place_of, tiles * SLOTS, 0)
    at = 0
    for part in parts:
        held[at : at + part.shape[0]] = part[...]
        at += part.shape[0]
    acc[...] = jnp.zeros_like(acc) if start else before[...]

    def some(g, carry):
        wait_slots(g, count, feet, buf, sems, slot_of)
        for k in range(UNROLL):
            j = g * UNROLL + k
            rows = pl.ds(pl.multiple_of(place_of[j] * CBLK, CBLK), CBLK)
            acc[slot_of[j] // SLOTS] += jnp.dot(
                buf[j], held[rows, :], preferred_element_type=f32
            )
        return carry

    lax.fori_loop(0, (count + UNROLL - 1) // UNROLL, some, 0)
    if end:
        keep[...] = movie[...].astype(f32) - acc[:tiles, :, :FR]
        send[...] = acc[:tiles, :, FR:].astype(bf16)


def rebuild(feet, places, parts, movie=None, before=None):
    slots = places.shape[0]
    tiles = slots // SLOTS
    room = slots + UNROLL
    blocks = sum(part.shape[0] for part in parts) // CBLK
    vmem = pl.BlockSpec(memory_space=pltpu.VMEM)
    extra = [v for v in (movie, before) if v is not None]
    running = (tiles + 1, TILE, WIDE)
    scratch = [
        pltpu.SMEM((room,), jnp.int32),
        pltpu.SMEM((room,), jnp.int32),
        pltpu.VMEM((blocks * CBLK, WIDE), bf16),
        pltpu.VMEM((room, TILE, CBLK), bf16),
        pltpu.SemaphoreType.DMA((slots,)),
    ]
    if movie is None:
        outs = [jax.ShapeDtypeStruct(running, f32)]
    else:
        outs = [
            jax.ShapeDtypeStruct((tiles, TILE, FR), f32),
            jax.ShapeDtypeStruct((tiles, TILE, FR), bf16),
        ]
        scratch = [pltpu.VMEM(running, f32)] + scratch
    return pl.pallas_call(
        functools.partial(
            rebuild_kernel, n_parts=len(parts), start=before is None, end=movie is not None
        ),
        in_specs=[
            pl.BlockSpec(memory_space=pltpu.SMEM),
            pl.BlockSpec(memory_space=pltpu.HBM),
        ]
        + [vmem] * (len(parts) + len(extra)),
        out_specs=[vmem] * len(outs),
        scratch_shapes=scratch,
        out_shape=outs,
        compiler_params=pltpu.CompilerParams(vmem_limit_bytes=45 * 2**20),
        cost_estimate=pl.CostEstimate(
            flops=84000000 * blocks, bytes_accessed=900000 * blocks, transcendentals=0
        ),
    )(places, feet, *parts, *extra)


def finish_kernel(keep, got, out):
    out[...] = (keep[...] - got[...].astype(f32)).astype(bf16)


def finish(keep, got):
    vmem = pl.BlockSpec(memory_space=pltpu.VMEM)
    return pl.pallas_call(
        finish_kernel,
        in_specs=[vmem, vmem],
        out_specs=vmem,
        out_shape=jax.ShapeDtypeStruct(got.shape, bf16),
        compiler_params=pltpu.CompilerParams(vmem_limit_bytes=8 * 2**20),
        cost_estimate=pl.CostEstimate(flops=700000, bytes_accessed=2600000, transcendentals=0),
    )(keep, got)


def shift(v, first, k):
    nz = lax.axis_size("z")
    pairs = []
    for y in range(SIDE):
        for x in range(SIDE):
            for z in range(nz):
                for c in range(2):
                    along_y = (c == 0) == first
                    ty, tx = ((y + k) % SIDE, x) if along_y else (y, (x + k) % SIDE)
                    pairs.append(
                        (((y * SIDE + x) * nz + z) * 2 + c, ((ty * SIDE + tx) * nz + z) * 2 + c)
                    )
    return lax.ppermute(v, AXES, pairs)


def swap(v):
    return lax.ppermute(v, "c", [(0, 1), (1, 0)])


def add(*terms):
    total = terms[0].astype(f32)
    for term in terms[1:]:
        total = total + term.astype(f32)
    return total.astype(bf16)


def reduce_plane(weighted, other, feet, soon, later):
    far_lo, far_hi, own_far, up_far, down_far = project(
        weighted, other, feet, soon, (2, 2, 1, 1, 1)
    )
    far_up = shift(far_lo, True, 1)
    far_down = shift(far_hi, True, -1)
    got_up_far = shift(up_far, True, 1)
    got_down_far = shift(add(down_far, far_down[CBLK:]), True, -1)
    own, up_lo, up_mid, down_lo, down_mid = project(
        weighted, other, feet, later, (3, 2, 1, 2, 1)
    )
    down_lo, got_up_far, got_down_far = lax.optimization_barrier(
        (down_lo, got_up_far, got_down_far)
    )
    far = add(own_far, got_up_far, got_down_far)
    got_up = shift(jnp.concatenate([add(up_lo, far_up), up_mid], axis=0), True, 1)
    got_down = shift(
        jnp.concatenate([down_lo, add(down_mid, far_down[:CBLK])], axis=0), True, -1
    )
    got_far = shift(far, False, 2)
    rest = add(own, got_up, got_down)
    got_up = shift(rest[CBLK : 2 * CBLK], False, 1)
    got_down = shift(rest[2 * CBLK :], False, -1)
    return add(rest[:CBLK], got_far, got_up, got_down)


def gather_and_rebuild(own, feet, first, second, third, movie, traces):
    h = CBLK // 2
    up, far, down = shift(own, False, -1), shift(own, False, 2), shift(own, False, 1)
    up_own, down_own = shift(own, True, -1), shift(own, True, 1)
    up, far, down, up_own, down_own = lax.optimization_barrier((up, far, down, up_own, down_own))
    others = jnp.concatenate([up, far, down], axis=0)
    up_others, down_others = shift(others, True, -1), shift(others, True, 1)
    far_own_lo, far_own_hi = shift(down_own[:h], True, 1), shift(up_own[h:], True, -1)
    (sums,) = rebuild(feet, first, (own, others, up_own, down_own))
    up_others, down_others, far_own_lo, far_own_hi, sums = lax.optimization_barrier(
        (up_others, down_others, far_own_lo, far_own_hi, sums)
    )
    m = CBLK + h
    far_lo, far_hi = shift(down_others[:m], True, 1), shift(up_others[m:], True, -1)
    sums, traces = lax.optimization_barrier((sums, traces))
    (sums,) = rebuild(
        feet, second, (up_others, down_others, far_own_lo, far_own_hi), None, sums
    )
    keep, send = rebuild(feet, third, (far_lo, far_hi), movie, sums)
    return traces, finish(keep, swap(send))


def shards(movie, noise_weight, footprints, block_ids, band_width, precision_blocks):
    nz = lax.axis_size("z")
    c = lax.axis_index("c")
    tiles = movie.shape[0]
    soon, later, first, second, third = places_of(block_ids)
    feet = footprints.reshape(tiles * SLOTS, TILE, CBLK)
    weighted = (noise_weight[:, :, None] * movie.astype(f32)).astype(bf16)
    projected = reduce_plane(
        weighted, swap(weighted), feet, soon, later
    )
    regrouped = lax.all_to_all(projected.reshape(nz, CBLK // nz, WIDE), "z", 0, 0, tiled=True)
    filtered = band_filter(regrouped, band_width, precision_blocks)
    back = lax.all_to_all(filtered, "z", 0, 0, tiled=True).reshape(CBLK, WIDE)
    mine, theirs = back[:, :FR], swap(back[:, FR:])
    traces = jnp.where(
        c == 0, jnp.concatenate([mine, theirs], 0), jnp.concatenate([theirs, mine], 0)
    )
    return gather_and_rebuild(back, feet, first, second, third, movie, traces)


def solution(mesh):
    devices = mesh.devices.reshape(SIDE, SIDE, mesh.devices.shape[1] // 2, 2)
    grid = Mesh(devices, AXES)
    pix, tm = ("y", "x"), ("z", "c")
    return jax.shard_map(
        shards,
        mesh=grid,
        in_specs=(
            P(pix, None, tm),
            P(pix, None),
            P(pix, None, None, None),
            P(pix, None),
            P(),
            P(),
        ),
        out_specs=(P(pix, tm), P(pix, None, tm)),
        check_vma=False,
    )
```

```python
import functools

import jax
import jax.numpy as jnp
from jax import lax
from jax.experimental import pallas as pl
from jax.experimental.pallas import tpu as pltpu
from jax.sharding import Mesh
from jax.sharding import PartitionSpec as P

CBLK = 512
TILE = 128
SLOTS = 4
GROUP = 16
BMAX = 5
FR = 128
WIDE = 2 * FR
SIDE = 4
OWNED = SIDE * SIDE
f32 = jnp.float32
bf16 = jnp.bfloat16
UNROLL = 4
AXES = ("y", "x", "z", "c")


def places_of(block_ids):
    y, x, c = lax.axis_index("y"), lax.axis_index("x"), lax.axis_index("c")
    owner = block_ids >> 1
    dy, dx = ((owner >> 2) - y) & 3, ((owner & 3) - x) & 3
    i, j = jnp.where(c == 0, dy, dx).reshape(-1), jnp.where(c == 0, dx, dy).reshape(-1)
    mine = ((block_ids & 1) == c).reshape(-1)
    nj = j ^ (j >> 1)

    def part(where, at):
        return jnp.where(mine & where, at, -1)

    far = i == 2
    early = ((i == 1) & (j == 2)) | ((i == 3) & (j == 0))
    soon = part(far | early, jnp.where(far, nj, 4 + (i >> 1)))
    later = part(~far & ~early, nj + jnp.where(i == 0, 0, 4 + (i & 2)))
    first = part((i == 0) | (~far & (j == 0)), jnp.where(i == 0, j, 4 + (i >> 1)))
    second = part(jnp.where(far, j == 0, (i != 0) & (j != 0)), jnp.where(far, 6, (i >> 1) * 3 + j - 1))
    third = part(far & (j != 0), j - 1)
    return soon, later, first, second, third


def start_slots(places, feet, buf, sems, slot_of, place_of, spare_slot, spare_place):
    def scan(i, count):
        at = places[i]
        slot_of[count] = i
        place_of[count] = at

        @pl.when(at >= 0)
        def _():
            pltpu.make_async_copy(feet.at[i], buf.at[count], sems.at[count]).start()

        return count + (at >= 0).astype(jnp.int32)

    count = lax.fori_loop(0, places.shape[0], scan, 0, unroll=4)
    for k in range(UNROLL - 1):
        slot_of[count + k] = spare_slot
        place_of[count + k] = spare_place
    return count


def wait_slots(g, count, feet, buf, sems, slot_of):
    for k in range(UNROLL):
        j = g * UNROLL + k

        @pl.when(j < count)
        def _():
            pltpu.make_async_copy(feet.at[slot_of[j]], buf.at[j], sems.at[j]).wait()


def project_kernel(places, own, other, feet, *rest):
    outs = rest[:-5]
    slot_of, place_of, acc, buf, sems = rest[-5:]

    count = start_slots(places, feet, buf, sems, slot_of, place_of, 0, acc.shape[0] - 1)
    acc[...] = jnp.zeros_like(acc)

    def some(g, carry):
        wait_slots(g, count, feet, buf, sems, slot_of)
        for k in range(UNROLL):
            j = g * UNROLL + k
            i = slot_of[j]
            w = jnp.concatenate([own[i // SLOTS], other[i // SLOTS]], axis=1)
            acc[place_of[j]] += lax.dot_general(
                buf[j], w, (((0,), (0,)), ((), ())), preferred_element_type=f32
            )
        return carry

    lax.fori_loop(0, (count + UNROLL - 1) // UNROLL, some, 0)
    at = 0
    for out in outs:
        k = out.shape[0] // CBLK
        out[...] = acc[at : at + k].reshape(out.shape).astype(bf16)
        at += k


def project(own, other, feet, places, sizes):
    slots = places.shape[0]
    room = slots + UNROLL
    total = sum(sizes)
    vmem = pl.BlockSpec(memory_space=pltpu.VMEM)
    hbm = pl.BlockSpec(memory_space=pltpu.HBM)
    return pl.pallas_call(
        project_kernel,
        in_specs=[pl.BlockSpec(memory_space=pltpu.SMEM), vmem, vmem, hbm],
        out_specs=[vmem] * len(sizes),
        scratch_shapes=[
            pltpu.SMEM((room,), jnp.int32),
            pltpu.SMEM((room,), jnp.int32),
            pltpu.VMEM((total + 1, CBLK, WIDE), f32),
            pltpu.VMEM((room, TILE, CBLK), bf16),
            pltpu.SemaphoreType.DMA((slots,)),
        ],
        out_shape=[jax.ShapeDtypeStruct((k * CBLK, WIDE), bf16) for k in sizes],
        compiler_params=pltpu.CompilerParams(vmem_limit_bytes=45 * 2**20),
        cost_estimate=pl.CostEstimate(
            flops=84000000 * total, bytes_accessed=900000 * total, transcendentals=0
        ),
    )(places, own, other, feet)


def filter_kernel(bw, x, prec, out, pad, acc):
    nz, rows, _ = x.shape
    nb = 2 * nz
    per = rows // GROUP
    y, xx, z, c = (lax.axis_index(name) for name in AXES)
    base = (((y * SIDE + xx) * 2 + c) * nz + z) * per
    pad[:BMAX] = jnp.zeros((BMAX, rows, FR), bf16)
    pad[BMAX + nb :] = jnp.zeros((BMAX, rows, FR), bf16)
    for i in range(nz):
        pad[BMAX + 2 * i + c] = x[i, :, :FR]
        pad[BMAX + 2 * i + 1 - c] = x[i, :, FR:]
    reach = jnp.concatenate(
        [jnp.full((1, GROUP, FR), bw[base + g], jnp.int32) for g in range(per)], axis=1
    )
    for d in range(-BMAX, BMAX + 1):
        src = pad[BMAX + d : BMAX + d + nb].reshape(nb * rows, FR)
        term = jnp.dot(src, prec[d + BMAX], preferred_element_type=f32).reshape(nb, rows, FR)
        term = jnp.where(reach >= abs(d), term, 0.0)
        if d == -BMAX:
            acc[...] = term
        else:
            acc[...] += term
    for i in range(nz):
        out[i, :, :FR] = acc[2 * i + c].astype(bf16)
        out[i, :, FR:] = acc[2 * i + 1 - c].astype(bf16)


def band_filter(x, bw, prec):
    nz, rows, _ = x.shape
    vmem = pl.BlockSpec(memory_space=pltpu.VMEM)
    return pl.pallas_call(
        filter_kernel,
        in_specs=[pl.BlockSpec(memory_space=pltpu.SMEM), vmem, vmem],
        out_specs=vmem,
        out_shape=jax.ShapeDtypeStruct(x.shape, bf16),
        scratch_shapes=[
            pltpu.VMEM((2 * nz + 2 * BMAX, rows, FR), bf16),
            pltpu.VMEM((2 * nz, rows, FR), f32),
        ],
        compiler_params=pltpu.CompilerParams(vmem_limit_bytes=8 * 2**20),
        cost_estimate=pl.CostEstimate(flops=369000000, bytes_accessed=800000, transcendentals=0),
    )(bw, x, prec)


def rebuild_kernel(places, feet, *rest, n_parts, start, end):
    parts, rest = rest[:n_parts], rest[n_parts:]
    rest, (slot_of, place_of, held, buf, sems) = rest[:-5], rest[-5:]
    if end:
        movie, before, keep, send, acc = rest
    elif start:
        (acc,) = rest
    else:
        before, acc = rest
    tiles = acc.shape[0] - 1
    count = start_slots(places, feet, buf, sems, slot_of, place_of, tiles * SLOTS, 0)
    at = 0
    for part in parts:
        held[at : at + part.shape[0]] = part[...]
        at += part.shape[0]
    acc[...] = jnp.zeros_like(acc) if start else before[...]

    def some(g, carry):
        wait_slots(g, count, feet, buf, sems, slot_of)
        for k in range(UNROLL):
            j = g * UNROLL + k
            rows = pl.ds(pl.multiple_of(place_of[j] * CBLK, CBLK), CBLK)
            acc[slot_of[j] // SLOTS] += jnp.dot(
                buf[j], held[rows, :], preferred_element_type=f32
            )
        return carry

    lax.fori_loop(0, (count + UNROLL - 1) // UNROLL, some, 0)
    if end:
        keep[...] = movie[...].astype(f32) - acc[:tiles, :, :FR]
        send[...] = acc[:tiles, :, FR:].astype(bf16)


def rebuild(feet, places, parts, movie=None, before=None):
    slots = places.shape[0]
    tiles = slots // SLOTS
    room = slots + UNROLL
    blocks = sum(part.shape[0] for part in parts) // CBLK
    vmem = pl.BlockSpec(memory_space=pltpu.VMEM)
    extra = [v for v in (movie, before) if v is not None]
    running = (tiles + 1, TILE, WIDE)
    scratch = [
        pltpu.SMEM((room,), jnp.int32),
        pltpu.SMEM((room,), jnp.int32),
        pltpu.VMEM((blocks * CBLK, WIDE), bf16),
        pltpu.VMEM((room, TILE, CBLK), bf16),
        pltpu.SemaphoreType.DMA((slots,)),
    ]
    if movie is None:
        outs = [jax.ShapeDtypeStruct(running, f32)]
    else:
        outs = [
            jax.ShapeDtypeStruct((tiles, TILE, FR), f32),
            jax.ShapeDtypeStruct((tiles, TILE, FR), bf16),
        ]
        scratch = [pltpu.VMEM(running, f32)] + scratch
    return pl.pallas_call(
        functools.partial(
            rebuild_kernel, n_parts=len(parts), start=before is None, end=movie is not None
        ),
        in_specs=[
            pl.BlockSpec(memory_space=pltpu.SMEM),
            pl.BlockSpec(memory_space=pltpu.HBM),
        ]
        + [vmem] * (len(parts) + len(extra)),
        out_specs=[vmem] * len(outs),
        scratch_shapes=scratch,
        out_shape=outs,
        compiler_params=pltpu.CompilerParams(vmem_limit_bytes=45 * 2**20),
        cost_estimate=pl.CostEstimate(
            flops=84000000 * blocks, bytes_accessed=900000 * blocks, transcendentals=0
        ),
    )(places, feet, *parts, *extra)


def finish_kernel(keep, got, out):
    out[...] = (keep[...] - got[...].astype(f32)).astype(bf16)


def finish(keep, got):
    vmem = pl.BlockSpec(memory_space=pltpu.VMEM)
    return pl.pallas_call(
        finish_kernel,
        in_specs=[vmem, vmem],
        out_specs=vmem,
        out_shape=jax.ShapeDtypeStruct(got.shape, bf16),
        compiler_params=pltpu.CompilerParams(vmem_limit_bytes=8 * 2**20),
        cost_estimate=pl.CostEstimate(flops=700000, bytes_accessed=2600000, transcendentals=0),
    )(keep, got)


def shift(v, first, k):
    nz = lax.axis_size("z")
    pairs = []
    for y in range(SIDE):
        for x in range(SIDE):
            for z in range(nz):
                for c in range(2):
                    along_y = (c == 0) == first
                    ty, tx = ((y + k) % SIDE, x) if along_y else (y, (x + k) % SIDE)
                    pairs.append(
                        (((y * SIDE + x) * nz + z) * 2 + c, ((ty * SIDE + tx) * nz + z) * 2 + c)
                    )
    return lax.ppermute(v, AXES, pairs)


def swap(v):
    return lax.ppermute(v, "c", [(0, 1), (1, 0)])


def add(*terms):
    total = terms[0].astype(f32)
    for term in terms[1:]:
        total = total + term.astype(f32)
    return total.astype(bf16)


def reduce_plane(weighted, other, feet, soon, later):
    far_lo, far_hi, up_far, down_own = project(weighted, other, feet, soon, (2, 2, 1, 1))
    far_up = shift(far_lo, True, 1)
    far_down = shift(far_hi, True, -1)
    got_up_far = shift(up_far, True, 1)
    got_down_own = shift(down_own, True, -1)
    own_own, own_near, own_far, up_own, up_up, up_down, down_up, down_rest = project(
        weighted, other, feet, later, (1, 2, 1, 1, 1, 1, 1, 2)
    )
    down_all = jnp.concatenate([down_up, add(down_rest, far_down)], axis=0)
    got_down = shift(down_all, True, -1)
    up_up, got_up_far, got_down_own = lax.optimization_barrier((up_up, got_up_far, got_down_own))
    got_up = shift(jnp.concatenate([add(up_up, far_up[CBLK:]), up_down], axis=0), True, 1)
    got_up_own = shift(add(up_own, far_up[:CBLK]), True, 1)
    near = add(own_near, got_up, got_down[: 2 * CBLK])
    far = add(own_far, got_up_far, got_down[2 * CBLK :])
    from_far = shift(far, False, 2)
    from_up = shift(near[:CBLK], False, 1)
    from_down = shift(near[CBLK:], False, -1)
    return add(own_own, got_up_own, got_down_own, from_far, from_up, from_down)


def gather_and_rebuild(own, feet, first, second, third, movie):
    h = CBLK // 2
    up, far, down = shift(own, False, -1), shift(own, False, 2), shift(own, False, 1)
    up_own, down_own = shift(own, True, -1), shift(own, True, 1)
    up, far, down, up_own, down_own = lax.optimization_barrier((up, far, down, up_own, down_own))
    one = jnp.concatenate([up, far[:h]], axis=0)
    two = jnp.concatenate([far[h:], down], axis=0)
    down_one, up_two = shift(one, True, 1), shift(two, True, -1)
    down_two, up_one = shift(two, True, 1), shift(one, True, -1)
    far_own_lo, far_own_hi = shift(down_own[:h], True, 1), shift(up_own[h:], True, -1)
    (sums,) = rebuild(feet, first, (own, one, two, up_own, down_own))
    down_one, up_two, far_own_lo, far_own_hi, sums, own = lax.optimization_barrier(
        (down_one, up_two, far_own_lo, far_own_hi, sums, own)
    )
    far_lo, far_hi = shift(down_one, True, 1), shift(up_two, True, -1)
    mine, theirs = own[:, :FR], swap(own[:, FR:])
    traces = jnp.where(
        lax.axis_index("c") == 0,
        jnp.concatenate([mine, theirs], 0),
        jnp.concatenate([theirs, mine], 0),
    )
    sums, traces = lax.optimization_barrier((sums, traces))
    (sums,) = rebuild(
        feet, second, (up_one, up_two, down_one, down_two, far_own_lo, far_own_hi), None, sums
    )
    keep, send = rebuild(feet, third, (far_lo, far_hi), movie, sums)
    return traces, finish(keep, swap(send))


def shards(movie, noise_weight, footprints, block_ids, band_width, precision_blocks):
    nz = lax.axis_size("z")
    tiles = movie.shape[0]
    soon, later, first, second, third = places_of(block_ids)
    feet = footprints.reshape(tiles * SLOTS, TILE, CBLK)
    weighted = (noise_weight[:, :, None] * movie.astype(f32)).astype(bf16)
    projected = reduce_plane(
        weighted, swap(weighted), feet, soon, later
    )
    regrouped = lax.all_to_all(projected.reshape(nz, CBLK // nz, WIDE), "z", 0, 0, tiled=True)
    filtered = band_filter(regrouped, band_width, precision_blocks)
    back = lax.all_to_all(filtered, "z", 0, 0, tiled=True).reshape(CBLK, WIDE)
    return gather_and_rebuild(back, feet, first, second, third, movie)


def solution(mesh):
    devices = mesh.devices.reshape(SIDE, SIDE, mesh.devices.shape[1] // 2, 2)
    grid = Mesh(devices, AXES)
    pix, tm = ("y", "x"), ("z", "c")
    return jax.shard_map(
        shards,
        mesh=grid,
        in_specs=(
            P(pix, None, tm),
            P(pix, None),
            P(pix, None, None, None),
            P(pix, None),
            P(),
            P(),
        ),
        out_specs=(P(pix, tm), P(pix, None, tm)),
        check_vma=False,
    )
```

```python
import functools

import jax
import jax.numpy as jnp
from jax import lax
from jax.experimental import pallas as pl
from jax.experimental.pallas import tpu as pltpu
from jax.sharding import Mesh
from jax.sharding import PartitionSpec as P

CBLK = 512
TILE = 128
SLOTS = 4
GROUP = 16
BMAX = 5
FR = 128
WIDE = 2 * FR
SIDE = 4
OWNED = SIDE * SIDE
f32 = jnp.float32
bf16 = jnp.bfloat16
UNROLL = 4
AXES = ("y", "x", "z", "c")


def places_of(block_ids):
    y, x, c = lax.axis_index("y"), lax.axis_index("x"), lax.axis_index("c")
    ids = lax.optimization_barrier(block_ids.reshape(-1))
    owner = ids >> 1
    dy, dx = ((owner >> 2) - y) & 3, ((owner & 3) - x) & 3
    i, j = jnp.where(c == 0, dy, dx), jnp.where(c == 0, dx, dy)
    mine = (ids & 1) == c
    nj = j ^ (j >> 1)

    def part(where, at):
        return jnp.where(mine & where, at, -1)

    far = i == 2
    early = ((i == 1) & (j == 2)) | ((i == 3) & (j == 0))
    soon = part(far | early, jnp.where(far, nj, 4 + (i >> 1)))
    later = part(~far & ~early, nj + jnp.where(i == 0, 0, 4 + (i & 2)))
    first, second, third = part(i == 0, j), part((i & 1) == 1, (i & 2) * 2 + j), part(far, j)
    return soon, later, first, second, third


def start_slots(places, feet, buf, sems, slot_of, place_of, spare_slot, spare_place):
    def scan(i, count):
        at = places[i]
        slot_of[count] = i
        place_of[count] = at

        @pl.when(at >= 0)
        def _():
            pltpu.make_async_copy(feet.at[i], buf.at[count], sems.at[count]).start()

        return count + (at >= 0).astype(jnp.int32)

    count = lax.fori_loop(0, places.shape[0], scan, 0, unroll=4)
    for k in range(UNROLL - 1):
        slot_of[count + k] = spare_slot
        place_of[count + k] = spare_place
    return count


def wait_slots(g, count, feet, buf, sems, slot_of):
    for k in range(UNROLL):
        j = g * UNROLL + k

        @pl.when(j < count)
        def _():
            pltpu.make_async_copy(feet.at[slot_of[j]], buf.at[j], sems.at[j]).wait()


def project_kernel(places, own, other, feet, *rest):
    outs = rest[:-5]
    slot_of, place_of, acc, buf, sems = rest[-5:]

    count = start_slots(places, feet, buf, sems, slot_of, place_of, 0, acc.shape[0] - 1)
    acc[...] = jnp.zeros_like(acc)

    def some(g, carry):
        wait_slots(g, count, feet, buf, sems, slot_of)
        for k in range(UNROLL):
            j = g * UNROLL + k
            i = slot_of[j]
            w = jnp.concatenate([own[i // SLOTS], other[i // SLOTS]], axis=1)
            acc[place_of[j]] += lax.dot_general(
                buf[j], w, (((0,), (0,)), ((), ())), preferred_element_type=f32
            )
        return carry

    lax.fori_loop(0, (count + UNROLL - 1) // UNROLL, some, 0)
    at = 0
    for out in outs:
        k = out.shape[0] // CBLK
        out[...] = acc[at : at + k].reshape(out.shape).astype(bf16)
        at += k


def project(own, other, feet, places, sizes):
    slots = places.shape[0]
    room = slots + UNROLL
    total = sum(sizes)
    vmem = pl.BlockSpec(memory_space=pltpu.VMEM)
    hbm = pl.BlockSpec(memory_space=pltpu.HBM)
    return pl.pallas_call(
        project_kernel,
        in_specs=[pl.BlockSpec(memory_space=pltpu.SMEM), vmem, vmem, hbm],
        out_specs=[vmem] * len(sizes),
        scratch_shapes=[
            pltpu.SMEM((room,), jnp.int32),
            pltpu.SMEM((room,), jnp.int32),
            pltpu.VMEM((total + 1, CBLK, WIDE), f32),
            pltpu.VMEM((room, TILE, CBLK), bf16),
            pltpu.SemaphoreType.DMA((slots,)),
        ],
        out_shape=[jax.ShapeDtypeStruct((k * CBLK, WIDE), bf16) for k in sizes],
        compiler_params=pltpu.CompilerParams(vmem_limit_bytes=45 * 2**20),
        cost_estimate=pl.CostEstimate(
            flops=84000000 * total, bytes_accessed=900000 * total, transcendentals=0
        ),
    )(places, own, other, feet)


def filter_kernel(bw, x, prec, out, pad, acc):
    nz, rows, _ = x.shape
    nb = 2 * nz
    per = rows // GROUP
    y, xx, z, c = (lax.axis_index(name) for name in AXES)
    base = (((y * SIDE + xx) * 2 + c) * nz + z) * per
    pad[:BMAX] = jnp.zeros((BMAX, rows, FR), bf16)
    pad[BMAX + nb :] = jnp.zeros((BMAX, rows, FR), bf16)
    for i in range(nz):
        pad[BMAX + 2 * i + c] = x[i, :, :FR]
        pad[BMAX + 2 * i + 1 - c] = x[i, :, FR:]
    reach = jnp.concatenate(
        [jnp.full((1, GROUP, FR), bw[base + g], jnp.int32) for g in range(per)], axis=1
    )
    for d in range(-BMAX, BMAX + 1):
        src = pad[BMAX + d : BMAX + d + nb].reshape(nb * rows, FR)
        term = jnp.dot(src, prec[d + BMAX], preferred_element_type=f32).reshape(nb, rows, FR)
        term = jnp.where(reach >= abs(d), term, 0.0)
        if d == -BMAX:
            acc[...] = term
        else:
            acc[...] += term
    for i in range(nz):
        out[i, :, :FR] = acc[2 * i + c].astype(bf16)
        out[i, :, FR:] = acc[2 * i + 1 - c].astype(bf16)


def band_filter(x, bw, prec):
    nz, rows, _ = x.shape
    vmem = pl.BlockSpec(memory_space=pltpu.VMEM)
    return pl.pallas_call(
        filter_kernel,
        in_specs=[pl.BlockSpec(memory_space=pltpu.SMEM), vmem, vmem],
        out_specs=vmem,
        out_shape=jax.ShapeDtypeStruct(x.shape, bf16),
        scratch_shapes=[
            pltpu.VMEM((2 * nz + 2 * BMAX, rows, FR), bf16),
            pltpu.VMEM((2 * nz, rows, FR), f32),
        ],
        compiler_params=pltpu.CompilerParams(vmem_limit_bytes=8 * 2**20),
        cost_estimate=pl.CostEstimate(flops=369000000, bytes_accessed=800000, transcendentals=0),
    )(bw, x, prec)


def rebuild_kernel(places, feet, *rest, n_parts, start, end):
    parts, rest = rest[:n_parts], rest[n_parts:]
    rest, (slot_of, place_of, held, buf, sems) = rest[:-5], rest[-5:]
    if end:
        movie, before, keep, send, acc = rest
    elif start:
        (acc,) = rest
    else:
        before, acc = rest
    tiles = acc.shape[0] - 1
    count = start_slots(places, feet, buf, sems, slot_of, place_of, tiles * SLOTS, 0)
    at = 0
    for part in parts:
        held[at : at + part.shape[0]] = part[...]
        at += part.shape[0]
    acc[...] = jnp.zeros_like(acc) if start else before[...]

    def some(g, carry):
        wait_slots(g, count, feet, buf, sems, slot_of)
        for k in range(UNROLL):
            j = g * UNROLL + k
            rows = pl.ds(pl.multiple_of(place_of[j] * CBLK, CBLK), CBLK)
            acc[slot_of[j] // SLOTS] += jnp.dot(
                buf[j], held[rows, :], preferred_element_type=f32
            )
        return carry

    lax.fori_loop(0, (count + UNROLL - 1) // UNROLL, some, 0)
    if end:
        keep[...] = movie[...].astype(f32) - acc[:tiles, :, :FR]
        send[...] = acc[:tiles, :, FR:].astype(bf16)


def rebuild(feet, places, parts, movie=None, before=None):
    slots = places.shape[0]
    tiles = slots // SLOTS
    room = slots + UNROLL
    blocks = sum(part.shape[0] for part in parts) // CBLK
    vmem = pl.BlockSpec(memory_space=pltpu.VMEM)
    extra = [v for v in (movie, before) if v is not None]
    running = (tiles + 1, TILE, WIDE)
    scratch = [
        pltpu.SMEM((room,), jnp.int32),
        pltpu.SMEM((room,), jnp.int32),
        pltpu.VMEM((blocks * CBLK, WIDE), bf16),
        pltpu.VMEM((room, TILE, CBLK), bf16),
        pltpu.SemaphoreType.DMA((slots,)),
    ]
    if movie is None:
        outs = [jax.ShapeDtypeStruct(running, f32)]
    else:
        outs = [
            jax.ShapeDtypeStruct((tiles, TILE, FR), f32),
            jax.ShapeDtypeStruct((tiles, TILE, FR), bf16),
        ]
        scratch = [pltpu.VMEM(running, f32)] + scratch
    return pl.pallas_call(
        functools.partial(
            rebuild_kernel, n_parts=len(parts), start=before is None, end=movie is not None
        ),
        in_specs=[
            pl.BlockSpec(memory_space=pltpu.SMEM),
            pl.BlockSpec(memory_space=pltpu.HBM),
        ]
        + [vmem] * (len(parts) + len(extra)),
        out_specs=[vmem] * len(outs),
        scratch_shapes=scratch,
        out_shape=outs,
        compiler_params=pltpu.CompilerParams(vmem_limit_bytes=45 * 2**20),
        cost_estimate=pl.CostEstimate(
            flops=84000000 * blocks, bytes_accessed=900000 * blocks, transcendentals=0
        ),
    )(places, feet, *parts, *extra)


def finish_kernel(keep, got, out):
    out[...] = (keep[...] - got[...].astype(f32)).astype(bf16)


def finish(keep, got):
    vmem = pl.BlockSpec(memory_space=pltpu.VMEM)
    return pl.pallas_call(
        finish_kernel,
        in_specs=[vmem, vmem],
        out_specs=vmem,
        out_shape=jax.ShapeDtypeStruct(got.shape, bf16),
        compiler_params=pltpu.CompilerParams(vmem_limit_bytes=8 * 2**20),
        cost_estimate=pl.CostEstimate(flops=700000, bytes_accessed=2600000, transcendentals=0),
    )(keep, got)


def shift(v, first, k):
    nz = lax.axis_size("z")
    pairs = []
    for y in range(SIDE):
        for x in range(SIDE):
            for z in range(nz):
                for c in range(2):
                    along_y = (c == 0) == first
                    ty, tx = ((y + k) % SIDE, x) if along_y else (y, (x + k) % SIDE)
                    pairs.append(
                        (((y * SIDE + x) * nz + z) * 2 + c, ((ty * SIDE + tx) * nz + z) * 2 + c)
                    )
    return lax.ppermute(v, AXES, pairs)


def swap(v):
    return lax.ppermute(v, "c", [(0, 1), (1, 0)])


def add(*terms):
    total = terms[0].astype(f32)
    for term in terms[1:]:
        total = total + term.astype(f32)
    return total.astype(bf16)


def reduce_plane(weighted, other, feet, soon, later):
    far_lo, far_hi, up_far, down_own = project(weighted, other, feet, soon, (2, 2, 1, 1))
    far_up = shift(far_lo, True, 1)
    far_down = shift(far_hi, True, -1)
    got_up_far = shift(up_far, True, 1)
    got_down_own = shift(down_own, True, -1)
    own_own, own_near, own_far, up_own, up_up, up_down, down_up, down_rest = project(
        weighted, other, feet, later, (1, 2, 1, 1, 1, 1, 1, 2)
    )
    down_all = jnp.concatenate([down_up, add(down_rest, far_down)], axis=0)
    got_down = shift(down_all, True, -1)
    up_up, got_up_far, got_down_own = lax.optimization_barrier((up_up, got_up_far, got_down_own))
    got_up = shift(jnp.concatenate([add(up_up, far_up[CBLK:]), up_down], axis=0), True, 1)
    got_up_own = shift(add(up_own, far_up[:CBLK]), True, 1)
    near = add(own_near, got_up, got_down[: 2 * CBLK])
    far = add(own_far, got_up_far, got_down[2 * CBLK :])
    from_far = shift(far, False, 2)
    from_up = shift(near[:CBLK], False, 1)
    from_down = shift(near[CBLK:], False, -1)
    return add(own_own, got_up_own, got_down_own, from_far, from_up, from_down)


def gather_and_rebuild(own, feet, first, second, third, movie):
    up, far, down = shift(own, False, -1), shift(own, False, 2), shift(own, False, 1)
    one = jnp.concatenate([own, up], axis=0)
    two = jnp.concatenate([far, down], axis=0)
    down_one, up_two = shift(one, True, 1), shift(two, True, -1)
    down_two, up_one = shift(two, True, 1), shift(one, True, -1)
    (sums,) = rebuild(feet, first, (one, two))
    down_one, up_two, sums, own = lax.optimization_barrier((down_one, up_two, sums, own))
    far_one, far_two = shift(down_one, True, 1), shift(up_two, True, -1)
    mine, theirs = own[:, :FR], swap(own[:, FR:])
    traces = jnp.where(
        lax.axis_index("c") == 0,
        jnp.concatenate([mine, theirs], 0),
        jnp.concatenate([theirs, mine], 0),
    )
    sums, traces = lax.optimization_barrier((sums, traces))
    (sums,) = rebuild(feet, second, (up_one, up_two, down_one, down_two), None, sums)
    keep, send = rebuild(feet, third, (far_one, far_two), movie, sums)
    return traces, finish(keep, swap(send))


def shards(movie, noise_weight, footprints, block_ids, band_width, precision_blocks):
    nz = lax.axis_size("z")
    tiles = movie.shape[0]
    soon, later, first, second, third = places_of(block_ids)
    feet = footprints.reshape(tiles * SLOTS, TILE, CBLK)
    weighted = (noise_weight[:, :, None] * movie.astype(f32)).astype(bf16)
    projected = reduce_plane(
        weighted, swap(weighted), feet, soon, later
    )
    regrouped = lax.all_to_all(projected.reshape(nz, CBLK // nz, WIDE), "z", 0, 0, tiled=True)
    filtered = band_filter(regrouped, band_width, precision_blocks)
    back = lax.all_to_all(filtered, "z", 0, 0, tiled=True).reshape(CBLK, WIDE)
    return gather_and_rebuild(back, feet, first, second, third, movie)


def solution(mesh):
    devices = mesh.devices.reshape(SIDE, SIDE, mesh.devices.shape[1] // 2, 2)
    grid = Mesh(devices, AXES)
    pix, tm = ("y", "x"), ("z", "c")
    return jax.shard_map(
        shards,
        mesh=grid,
        in_specs=(
            P(pix, None, tm),
            P(pix, None),
            P(pix, None, None, None),
            P(pix, None),
            P(),
            P(),
        ),
        out_specs=(P(pix, tm), P(pix, None, tm)),
        check_vma=False,
    )
```

```python
import functools

import jax
import jax.numpy as jnp
from jax import lax
from jax.experimental import pallas as pl
from jax.experimental.pallas import tpu as pltpu
from jax.sharding import Mesh
from jax.sharding import PartitionSpec as P

CBLK = 512
TILE = 128
SLOTS = 4
GROUP = 16
BMAX = 5
FR = 128
WIDE = 2 * FR
SIDE = 4
OWNED = SIDE * SIDE
f32 = jnp.float32
bf16 = jnp.bfloat16
UNROLL = 4
AXES = ("y", "x", "z", "c")


def places_of(block_ids):
    y, x, c = lax.axis_index("y"), lax.axis_index("x"), lax.axis_index("c")
    ids = lax.optimization_barrier(block_ids.reshape(-1))
    owner = ids >> 1
    dy, dx = ((owner >> 2) - y) & 3, ((owner & 3) - x) & 3
    i, j = jnp.where(c == 0, dy, dx), jnp.where(c == 0, dx, dy)
    mine = (ids & 1) == c
    nj = j ^ (j >> 1)

    def part(where, at):
        return jnp.where(mine & where, at, -1)

    far = i == 2
    soon, later = part(far, nj), part(~far, nj + (i & 1) * 4 + (i & 2) * 2)
    first, second, third = part(i == 0, j), part((i & 1) == 1, (i & 2) * 2 + j), part(far, j)
    return soon, later, first, second, third


def start_slots(places, feet, buf, sems, slot_of, place_of, spare_slot, spare_place):
    def scan(i, count):
        at = places[i]
        slot_of[count] = i
        place_of[count] = at

        @pl.when(at >= 0)
        def _():
            pltpu.make_async_copy(feet.at[i], buf.at[count], sems.at[count]).start()

        return count + (at >= 0).astype(jnp.int32)

    count = lax.fori_loop(0, places.shape[0], scan, 0, unroll=4)
    for k in range(UNROLL - 1):
        slot_of[count + k] = spare_slot
        place_of[count + k] = spare_place
    return count


def wait_slots(g, count, feet, buf, sems, slot_of):
    for k in range(UNROLL):
        j = g * UNROLL + k

        @pl.when(j < count)
        def _():
            pltpu.make_async_copy(feet.at[slot_of[j]], buf.at[j], sems.at[j]).wait()


def project_kernel(places, own, other, feet, *rest):
    outs = rest[:-5]
    slot_of, place_of, acc, buf, sems = rest[-5:]

    count = start_slots(places, feet, buf, sems, slot_of, place_of, 0, acc.shape[0] - 1)
    acc[...] = jnp.zeros_like(acc)

    def some(g, carry):
        wait_slots(g, count, feet, buf, sems, slot_of)
        for k in range(UNROLL):
            j = g * UNROLL + k
            i = slot_of[j]
            w = jnp.concatenate([own[i // SLOTS], other[i // SLOTS]], axis=1)
            acc[place_of[j]] += lax.dot_general(
                buf[j], w, (((0,), (0,)), ((), ())), preferred_element_type=f32
            )
        return carry

    lax.fori_loop(0, (count + UNROLL - 1) // UNROLL, some, 0)
    at = 0
    for out in outs:
        k = out.shape[0] // CBLK
        out[...] = acc[at : at + k].reshape(out.shape).astype(bf16)
        at += k


def project(own, other, feet, places, sizes):
    slots = places.shape[0]
    room = slots + UNROLL
    total = sum(sizes)
    vmem = pl.BlockSpec(memory_space=pltpu.VMEM)
    hbm = pl.BlockSpec(memory_space=pltpu.HBM)
    return pl.pallas_call(
        project_kernel,
        in_specs=[pl.BlockSpec(memory_space=pltpu.SMEM), vmem, vmem, hbm],
        out_specs=[vmem] * len(sizes),
        scratch_shapes=[
            pltpu.SMEM((room,), jnp.int32),
            pltpu.SMEM((room,), jnp.int32),
            pltpu.VMEM((total + 1, CBLK, WIDE), f32),
            pltpu.VMEM((room, TILE, CBLK), bf16),
            pltpu.SemaphoreType.DMA((slots,)),
        ],
        out_shape=[jax.ShapeDtypeStruct((k * CBLK, WIDE), bf16) for k in sizes],
        compiler_params=pltpu.CompilerParams(vmem_limit_bytes=45 * 2**20),
        cost_estimate=pl.CostEstimate(
            flops=84000000 * total, bytes_accessed=900000 * total, transcendentals=0
        ),
    )(places, own, other, feet)


def filter_kernel(bw, x, prec, out, pad, acc):
    nz, rows, _ = x.shape
    nb = 2 * nz
    per = rows // GROUP
    y, xx, z, c = (lax.axis_index(name) for name in AXES)
    base = (((y * SIDE + xx) * 2 + c) * nz + z) * per
    pad[:BMAX] = jnp.zeros((BMAX, rows, FR), bf16)
    pad[BMAX + nb :] = jnp.zeros((BMAX, rows, FR), bf16)
    for i in range(nz):
        pad[BMAX + 2 * i + c] = x[i, :, :FR]
        pad[BMAX + 2 * i + 1 - c] = x[i, :, FR:]
    reach = jnp.concatenate(
        [jnp.full((1, GROUP, FR), bw[base + g], jnp.int32) for g in range(per)], axis=1
    )
    for d in range(-BMAX, BMAX + 1):
        src = pad[BMAX + d : BMAX + d + nb].reshape(nb * rows, FR)
        term = jnp.dot(src, prec[d + BMAX], preferred_element_type=f32).reshape(nb, rows, FR)
        term = jnp.where(reach >= abs(d), term, 0.0)
        if d == -BMAX:
            acc[...] = term
        else:
            acc[...] += term
    for i in range(nz):
        out[i, :, :FR] = acc[2 * i + c].astype(bf16)
        out[i, :, FR:] = acc[2 * i + 1 - c].astype(bf16)


def band_filter(x, bw, prec):
    nz, rows, _ = x.shape
    vmem = pl.BlockSpec(memory_space=pltpu.VMEM)
    return pl.pallas_call(
        filter_kernel,
        in_specs=[pl.BlockSpec(memory_space=pltpu.SMEM), vmem, vmem],
        out_specs=vmem,
        out_shape=jax.ShapeDtypeStruct(x.shape, bf16),
        scratch_shapes=[
            pltpu.VMEM((2 * nz + 2 * BMAX, rows, FR), bf16),
            pltpu.VMEM((2 * nz, rows, FR), f32),
        ],
        compiler_params=pltpu.CompilerParams(vmem_limit_bytes=8 * 2**20),
        cost_estimate=pl.CostEstimate(flops=369000000, bytes_accessed=800000, transcendentals=0),
    )(bw, x, prec)


def rebuild_kernel(places, feet, *rest, n_parts, start, end):
    parts, rest = rest[:n_parts], rest[n_parts:]
    rest, (slot_of, place_of, held, buf, sems) = rest[:-5], rest[-5:]
    if end:
        movie, before, keep, send, acc = rest
    elif start:
        (acc,) = rest
    else:
        before, acc = rest
    tiles = acc.shape[0] - 1
    count = start_slots(places, feet, buf, sems, slot_of, place_of, tiles * SLOTS, 0)
    at = 0
    for part in parts:
        held[at : at + part.shape[0]] = part[...]
        at += part.shape[0]
    acc[...] = jnp.zeros_like(acc) if start else before[...]

    def some(g, carry):
        wait_slots(g, count, feet, buf, sems, slot_of)
        for k in range(UNROLL):
            j = g * UNROLL + k
            rows = pl.ds(pl.multiple_of(place_of[j] * CBLK, CBLK), CBLK)
            acc[slot_of[j] // SLOTS] += jnp.dot(
                buf[j], held[rows, :], preferred_element_type=f32
            )
        return carry

    lax.fori_loop(0, (count + UNROLL - 1) // UNROLL, some, 0)
    if end:
        keep[...] = movie[...].astype(f32) - acc[:tiles, :, :FR]
        send[...] = acc[:tiles, :, FR:].astype(bf16)


def rebuild(feet, places, parts, movie=None, before=None):
    slots = places.shape[0]
    tiles = slots // SLOTS
    room = slots + UNROLL
    blocks = sum(part.shape[0] for part in parts) // CBLK
    vmem = pl.BlockSpec(memory_space=pltpu.VMEM)
    extra = [v for v in (movie, before) if v is not None]
    running = (tiles + 1, TILE, WIDE)
    scratch = [
        pltpu.SMEM((room,), jnp.int32),
        pltpu.SMEM((room,), jnp.int32),
        pltpu.VMEM((blocks * CBLK, WIDE), bf16),
        pltpu.VMEM((room, TILE, CBLK), bf16),
        pltpu.SemaphoreType.DMA((slots,)),
    ]
    if movie is None:
        outs = [jax.ShapeDtypeStruct(running, f32)]
    else:
        outs = [
            jax.ShapeDtypeStruct((tiles, TILE, FR), f32),
            jax.ShapeDtypeStruct((tiles, TILE, FR), bf16),
        ]
        scratch = [pltpu.VMEM(running, f32)] + scratch
    return pl.pallas_call(
        functools.partial(
            rebuild_kernel, n_parts=len(parts), start=before is None, end=movie is not None
        ),
        in_specs=[
            pl.BlockSpec(memory_space=pltpu.SMEM),
            pl.BlockSpec(memory_space=pltpu.HBM),
        ]
        + [vmem] * (len(parts) + len(extra)),
        out_specs=[vmem] * len(outs),
        scratch_shapes=scratch,
        out_shape=outs,
        compiler_params=pltpu.CompilerParams(vmem_limit_bytes=45 * 2**20),
        cost_estimate=pl.CostEstimate(
            flops=84000000 * blocks, bytes_accessed=900000 * blocks, transcendentals=0
        ),
    )(places, feet, *parts, *extra)


def finish_kernel(keep, got, out):
    out[...] = (keep[...] - got[...].astype(f32)).astype(bf16)


def finish(keep, got):
    vmem = pl.BlockSpec(memory_space=pltpu.VMEM)
    return pl.pallas_call(
        finish_kernel,
        in_specs=[vmem, vmem],
        out_specs=vmem,
        out_shape=jax.ShapeDtypeStruct(got.shape, bf16),
        compiler_params=pltpu.CompilerParams(vmem_limit_bytes=8 * 2**20),
        cost_estimate=pl.CostEstimate(flops=700000, bytes_accessed=2600000, transcendentals=0),
    )(keep, got)


def shift(v, first, k):
    nz = lax.axis_size("z")
    pairs = []
    for y in range(SIDE):
        for x in range(SIDE):
            for z in range(nz):
                for c in range(2):
                    along_y = (c == 0) == first
                    ty, tx = ((y + k) % SIDE, x) if along_y else (y, (x + k) % SIDE)
                    pairs.append(
                        (((y * SIDE + x) * nz + z) * 2 + c, ((ty * SIDE + tx) * nz + z) * 2 + c)
                    )
    return lax.ppermute(v, AXES, pairs)


def swap(v):
    return lax.ppermute(v, "c", [(0, 1), (1, 0)])


def add(*terms):
    total = terms[0].astype(f32)
    for term in terms[1:]:
        total = total + term.astype(f32)
    return total.astype(bf16)


def reduce_plane(weighted, other, feet, soon, later):
    far_lo, far_hi = project(weighted, other, feet, soon, (2, 2))
    far_up = shift(far_lo, True, 1)
    far_down = shift(far_hi, True, -1)
    own_own, own_rest, up_own, up_up, up_rest, down_own, down_up, down_rest = project(
        weighted, other, feet, later, (1, 3, 1, 1, 2, 1, 1, 2)
    )
    down_all = jnp.concatenate([down_up, add(down_rest, far_down)], axis=0)
    up_all = jnp.concatenate([add(up_up, far_up[CBLK:]), up_rest], axis=0)
    got_down, got_up = shift(down_all, True, -1), shift(up_all, True, 1)
    got_up_own, got_down_own = shift(add(up_own, far_up[:CBLK]), True, 1), shift(down_own, True, -1)
    rest = add(own_rest, got_up, got_down)
    from_far = shift(rest[2 * CBLK :], False, 2)
    from_up = shift(rest[:CBLK], False, 1)
    from_down = shift(rest[CBLK : 2 * CBLK], False, -1)
    return add(own_own, got_up_own, got_down_own, from_far, from_up, from_down)


def gather_and_rebuild(own, feet, first, second, third, movie):
    up, far, down = shift(own, False, -1), shift(own, False, 2), shift(own, False, 1)
    one = jnp.concatenate([own, up], axis=0)
    two = jnp.concatenate([far, down], axis=0)
    down_one, up_two = shift(one, True, 1), shift(two, True, -1)
    down_two, up_one = shift(two, True, 1), shift(one, True, -1)
    (sums,) = rebuild(feet, first, (one, two))
    down_one, up_two, sums, own = lax.optimization_barrier((down_one, up_two, sums, own))
    far_one, far_two = shift(down_one, True, 1), shift(up_two, True, -1)
    mine, theirs = own[:, :FR], swap(own[:, FR:])
    traces = jnp.where(
        lax.axis_index("c") == 0,
        jnp.concatenate([mine, theirs], 0),
        jnp.concatenate([theirs, mine], 0),
    )
    sums, traces = lax.optimization_barrier((sums, traces))
    (sums,) = rebuild(feet, second, (up_one, up_two, down_one, down_two), None, sums)
    keep, send = rebuild(feet, third, (far_one, far_two), movie, sums)
    return traces, finish(keep, swap(send))


def shards(movie, noise_weight, footprints, block_ids, band_width, precision_blocks):
    nz = lax.axis_size("z")
    tiles = movie.shape[0]
    soon, later, first, second, third = places_of(block_ids)
    feet = footprints.reshape(tiles * SLOTS, TILE, CBLK)
    weighted = (noise_weight[:, :, None] * movie.astype(f32)).astype(bf16)
    projected = reduce_plane(
        weighted, swap(weighted), feet, soon, later
    )
    regrouped = lax.all_to_all(projected.reshape(nz, CBLK // nz, WIDE), "z", 0, 0, tiled=True)
    filtered = band_filter(regrouped, band_width, precision_blocks)
    back = lax.all_to_all(filtered, "z", 0, 0, tiled=True).reshape(CBLK, WIDE)
    return gather_and_rebuild(back, feet, first, second, third, movie)


def solution(mesh):
    devices = mesh.devices.reshape(SIDE, SIDE, mesh.devices.shape[1] // 2, 2)
    grid = Mesh(devices, AXES)
    pix, tm = ("y", "x"), ("z", "c")
    return jax.shard_map(
        shards,
        mesh=grid,
        in_specs=(
            P(pix, None, tm),
            P(pix, None),
            P(pix, None, None, None),
            P(pix, None),
            P(),
            P(),
        ),
        out_specs=(P(pix, tm), P(pix, None, tm)),
        check_vma=False,
    )
```

```python
import functools

import jax
import jax.numpy as jnp
from jax import lax
from jax.experimental import pallas as pl
from jax.experimental.pallas import tpu as pltpu
from jax.sharding import Mesh
from jax.sharding import PartitionSpec as P

CBLK = 512
TILE = 128
SLOTS = 4
GROUP = 16
BMAX = 5
FR = 128
WIDE = 2 * FR
SIDE = 4
OWNED = SIDE * SIDE
f32 = jnp.float32
bf16 = jnp.bfloat16
UNROLL = 6
AXES = ("y", "x", "z", "c")


def places_of(block_ids):
    y, x, c = lax.axis_index("y"), lax.axis_index("x"), lax.axis_index("c")
    ids = lax.optimization_barrier(block_ids.reshape(-1))
    owner = ids >> 1
    dy, dx = ((owner >> 2) - y) & 3, ((owner & 3) - x) & 3
    i, j = jnp.where(c == 0, dy, dx), jnp.where(c == 0, dx, dy)
    mine = (ids & 1) == c
    nj = j ^ (j >> 1)

    def part(where, at):
        return jnp.where(mine & where, at, -1)

    far = i == 2
    soon, later = part(far, nj), part(~far, nj + (i & 1) * 4 + (i & 2) * 2)
    first, second, third = part(i == 0, j), part((i & 1) == 1, (i & 2) * 2 + j), part(far, j)
    return soon, later, first, second, third


def start_slots(places, feet, buf, sems, slot_of, place_of, spare_slot, spare_place):
    def scan(i, count):
        at = places[i]
        slot_of[count] = i
        place_of[count] = at

        @pl.when(at >= 0)
        def _():
            pltpu.make_async_copy(feet.at[i], buf.at[count], sems.at[count]).start()

        return count + (at >= 0).astype(jnp.int32)

    count = lax.fori_loop(0, places.shape[0], scan, 0, unroll=4)
    for k in range(UNROLL - 1):
        slot_of[count + k] = spare_slot
        place_of[count + k] = spare_place
    return count


def wait_slots(g, count, feet, buf, sems, slot_of):
    for k in range(UNROLL):
        j = g * UNROLL + k

        @pl.when(j < count)
        def _():
            pltpu.make_async_copy(feet.at[slot_of[j]], buf.at[j], sems.at[j]).wait()


def project_kernel(places, own, other, feet, *rest):
    outs = rest[:-5]
    slot_of, place_of, acc, buf, sems = rest[-5:]

    count = start_slots(places, feet, buf, sems, slot_of, place_of, 0, acc.shape[0] - 1)
    acc[...] = jnp.zeros_like(acc)

    def some(g, carry):
        wait_slots(g, count, feet, buf, sems, slot_of)
        for k in range(UNROLL):
            j = g * UNROLL + k
            i = slot_of[j]
            w = jnp.concatenate([own[i // SLOTS], other[i // SLOTS]], axis=1)
            acc[place_of[j]] += lax.dot_general(
                buf[j], w, (((0,), (0,)), ((), ())), preferred_element_type=f32
            )
        return carry

    lax.fori_loop(0, (count + UNROLL - 1) // UNROLL, some, 0)
    at = 0
    for out in outs:
        k = out.shape[0] // CBLK
        out[...] = acc[at : at + k].reshape(out.shape).astype(bf16)
        at += k


def project(own, other, feet, places, sizes):
    slots = places.shape[0]
    room = slots + UNROLL
    total = sum(sizes)
    vmem = pl.BlockSpec(memory_space=pltpu.VMEM)
    hbm = pl.BlockSpec(memory_space=pltpu.HBM)
    return pl.pallas_call(
        project_kernel,
        in_specs=[pl.BlockSpec(memory_space=pltpu.SMEM), vmem, vmem, hbm],
        out_specs=[vmem] * len(sizes),
        scratch_shapes=[
            pltpu.SMEM((room,), jnp.int32),
            pltpu.SMEM((room,), jnp.int32),
            pltpu.VMEM((total + 1, CBLK, WIDE), f32),
            pltpu.VMEM((room, TILE, CBLK), bf16),
            pltpu.SemaphoreType.DMA((slots,)),
        ],
        out_shape=[jax.ShapeDtypeStruct((k * CBLK, WIDE), bf16) for k in sizes],
        compiler_params=pltpu.CompilerParams(vmem_limit_bytes=45 * 2**20),
        cost_estimate=pl.CostEstimate(
            flops=84000000 * total, bytes_accessed=900000 * total, transcendentals=0
        ),
    )(places, own, other, feet)


def filter_kernel(bw, x, prec, out, pad, acc):
    nz, rows, _ = x.shape
    nb = 2 * nz
    per = rows // GROUP
    y, xx, z, c = (lax.axis_index(name) for name in AXES)
    base = (((y * SIDE + xx) * 2 + c) * nz + z) * per
    pad[:BMAX] = jnp.zeros((BMAX, rows, FR), bf16)
    pad[BMAX + nb :] = jnp.zeros((BMAX, rows, FR), bf16)
    for i in range(nz):
        pad[BMAX + 2 * i + c] = x[i, :, :FR]
        pad[BMAX + 2 * i + 1 - c] = x[i, :, FR:]
    reach = jnp.concatenate(
        [jnp.full((1, GROUP, FR), bw[base + g], jnp.int32) for g in range(per)], axis=1
    )
    for d in range(-BMAX, BMAX + 1):
        src = pad[BMAX + d : BMAX + d + nb].reshape(nb * rows, FR)
        term = jnp.dot(src, prec[d + BMAX], preferred_element_type=f32).reshape(nb, rows, FR)
        term = jnp.where(reach >= abs(d), term, 0.0)
        if d == -BMAX:
            acc[...] = term
        else:
            acc[...] += term
    for i in range(nz):
        out[i, :, :FR] = acc[2 * i + c].astype(bf16)
        out[i, :, FR:] = acc[2 * i + 1 - c].astype(bf16)


def band_filter(x, bw, prec):
    nz, rows, _ = x.shape
    vmem = pl.BlockSpec(memory_space=pltpu.VMEM)
    return pl.pallas_call(
        filter_kernel,
        in_specs=[pl.BlockSpec(memory_space=pltpu.SMEM), vmem, vmem],
        out_specs=vmem,
        out_shape=jax.ShapeDtypeStruct(x.shape, bf16),
        scratch_shapes=[
            pltpu.VMEM((2 * nz + 2 * BMAX, rows, FR), bf16),
            pltpu.VMEM((2 * nz, rows, FR), f32),
        ],
        compiler_params=pltpu.CompilerParams(vmem_limit_bytes=8 * 2**20),
        cost_estimate=pl.CostEstimate(flops=369000000, bytes_accessed=800000, transcendentals=0),
    )(bw, x, prec)


def rebuild_kernel(places, feet, *rest, n_parts, start, end):
    parts, rest = rest[:n_parts], rest[n_parts:]
    rest, (slot_of, place_of, held, buf, sems) = rest[:-5], rest[-5:]
    if end:
        movie, before, keep, send, acc = rest
    elif start:
        (acc,) = rest
    else:
        before, acc = rest
    tiles = acc.shape[0] - 1
    count = start_slots(places, feet, buf, sems, slot_of, place_of, tiles * SLOTS, 0)
    at = 0
    for part in parts:
        held[at : at + part.shape[0]] = part[...]
        at += part.shape[0]
    acc[...] = jnp.zeros_like(acc) if start else before[...]

    def some(g, carry):
        wait_slots(g, count, feet, buf, sems, slot_of)
        for k in range(UNROLL):
            j = g * UNROLL + k
            rows = pl.ds(pl.multiple_of(place_of[j] * CBLK, CBLK), CBLK)
            acc[slot_of[j] // SLOTS] += jnp.dot(
                buf[j], held[rows, :], preferred_element_type=f32
            )
        return carry

    lax.fori_loop(0, (count + UNROLL - 1) // UNROLL, some, 0)
    if end:
        keep[...] = movie[...].astype(f32) - acc[:tiles, :, :FR]
        send[...] = acc[:tiles, :, FR:].astype(bf16)


def rebuild(feet, places, parts, movie=None, before=None):
    slots = places.shape[0]
    tiles = slots // SLOTS
    room = slots + UNROLL
    blocks = sum(part.shape[0] for part in parts) // CBLK
    vmem = pl.BlockSpec(memory_space=pltpu.VMEM)
    extra = [v for v in (movie, before) if v is not None]
    running = (tiles + 1, TILE, WIDE)
    scratch = [
        pltpu.SMEM((room,), jnp.int32),
        pltpu.SMEM((room,), jnp.int32),
        pltpu.VMEM((blocks * CBLK, WIDE), bf16),
        pltpu.VMEM((room, TILE, CBLK), bf16),
        pltpu.SemaphoreType.DMA((slots,)),
    ]
    if movie is None:
        outs = [jax.ShapeDtypeStruct(running, f32)]
    else:
        outs = [
            jax.ShapeDtypeStruct((tiles, TILE, FR), f32),
            jax.ShapeDtypeStruct((tiles, TILE, FR), bf16),
        ]
        scratch = [pltpu.VMEM(running, f32)] + scratch
    return pl.pallas_call(
        functools.partial(
            rebuild_kernel, n_parts=len(parts), start=before is None, end=movie is not None
        ),
        in_specs=[
            pl.BlockSpec(memory_space=pltpu.SMEM),
            pl.BlockSpec(memory_space=pltpu.HBM),
        ]
        + [vmem] * (len(parts) + len(extra)),
        out_specs=[vmem] * len(outs),
        scratch_shapes=scratch,
        out_shape=outs,
        compiler_params=pltpu.CompilerParams(vmem_limit_bytes=45 * 2**20),
        cost_estimate=pl.CostEstimate(
            flops=84000000 * blocks, bytes_accessed=900000 * blocks, transcendentals=0
        ),
    )(places, feet, *parts, *extra)


def finish_kernel(keep, got, out):
    out[...] = (keep[...] - got[...].astype(f32)).astype(bf16)


def finish(keep, got):
    vmem = pl.BlockSpec(memory_space=pltpu.VMEM)
    return pl.pallas_call(
        finish_kernel,
        in_specs=[vmem, vmem],
        out_specs=vmem,
        out_shape=jax.ShapeDtypeStruct(got.shape, bf16),
        compiler_params=pltpu.CompilerParams(vmem_limit_bytes=8 * 2**20),
        cost_estimate=pl.CostEstimate(flops=700000, bytes_accessed=2600000, transcendentals=0),
    )(keep, got)


def shift(v, first, k):
    nz = lax.axis_size("z")
    pairs = []
    for y in range(SIDE):
        for x in range(SIDE):
            for z in range(nz):
                for c in range(2):
                    along_y = (c == 0) == first
                    ty, tx = ((y + k) % SIDE, x) if along_y else (y, (x + k) % SIDE)
                    pairs.append(
                        (((y * SIDE + x) * nz + z) * 2 + c, ((ty * SIDE + tx) * nz + z) * 2 + c)
                    )
    return lax.ppermute(v, AXES, pairs)


def swap(v):
    return lax.ppermute(v, "c", [(0, 1), (1, 0)])


def add(*terms):
    total = terms[0].astype(f32)
    for term in terms[1:]:
        total = total + term.astype(f32)
    return total.astype(bf16)


def reduce_plane(weighted, other, feet, soon, later):
    far_lo, far_hi = project(weighted, other, feet, soon, (2, 2))
    far_up = shift(far_lo, True, 1)
    far_down = shift(far_hi, True, -1)
    own_own, own_up, own_down, own_far, up_own, up_up, up_rest, down_own, down_up, down_rest = (
        project(weighted, other, feet, later, (1, 1, 1, 1, 1, 1, 2, 1, 1, 2))
    )
    down_all = jnp.concatenate([down_up, add(down_rest, far_down)], axis=0)
    up_all = jnp.concatenate([add(up_up, far_up[CBLK:]), up_rest], axis=0)
    got_down, got_up = shift(down_all, True, -1), shift(up_all, True, 1)
    got_up_own, got_down_own = shift(add(up_own, far_up[:CBLK]), True, 1), shift(down_own, True, -1)
    n = CBLK
    from_far = shift(add(own_far, got_up[2 * n :], got_down[2 * n :]), False, 2)
    from_up = shift(add(own_up, got_up[:n], got_down[:n]), False, 1)
    from_down = shift(add(own_down, got_up[n : 2 * n], got_down[n : 2 * n]), False, -1)
    return add(own_own, got_up_own, got_down_own, from_far, from_up, from_down)


def gather_and_rebuild(own, feet, first, second, third, movie):
    up, far, down = shift(own, False, -1), shift(own, False, 2), shift(own, False, 1)
    one = jnp.concatenate([own, up], axis=0)
    two = jnp.concatenate([far, down], axis=0)
    down_one, up_two = shift(one, True, 1), shift(two, True, -1)
    down_two, up_one = shift(two, True, 1), shift(one, True, -1)
    (sums,) = rebuild(feet, first, (one, two))
    down_one, up_two, sums, own = lax.optimization_barrier((down_one, up_two, sums, own))
    far_one, far_two = shift(down_one, True, 1), shift(up_two, True, -1)
    mine, theirs = own[:, :FR], swap(own[:, FR:])
    traces = jnp.where(
        lax.axis_index("c") == 0,
        jnp.concatenate([mine, theirs], 0),
        jnp.concatenate([theirs, mine], 0),
    )
    sums, traces = lax.optimization_barrier((sums, traces))
    (sums,) = rebuild(feet, second, (up_one, up_two, down_one, down_two), None, sums)
    keep, send = rebuild(feet, third, (far_one, far_two), movie, sums)
    return traces, finish(keep, swap(send))


def shards(movie, noise_weight, footprints, block_ids, band_width, precision_blocks):
    nz = lax.axis_size("z")
    tiles = movie.shape[0]
    soon, later, first, second, third = places_of(block_ids)
    feet = footprints.reshape(tiles * SLOTS, TILE, CBLK)
    weighted = (noise_weight[:, :, None] * movie.astype(f32)).astype(bf16)
    projected = reduce_plane(
        weighted, swap(weighted), feet, soon, later
    )
    regrouped = lax.all_to_all(projected.reshape(nz, CBLK // nz, WIDE), "z", 0, 0, tiled=True)
    filtered = band_filter(regrouped, band_width, precision_blocks)
    back = lax.all_to_all(filtered, "z", 0, 0, tiled=True).reshape(CBLK, WIDE)
    return gather_and_rebuild(back, feet, first, second, third, movie)


def solution(mesh):
    devices = mesh.devices.reshape(SIDE, SIDE, mesh.devices.shape[1] // 2, 2)
    grid = Mesh(devices, AXES)
    pix, tm = ("y", "x"), ("z", "c")
    return jax.shard_map(
        shards,
        mesh=grid,
        in_specs=(
            P(pix, None, tm),
            P(pix, None),
            P(pix, None, None, None),
            P(pix, None),
            P(),
            P(),
        ),
        out_specs=(P(pix, tm), P(pix, None, tm)),
        check_vma=False,
    )
```
